32 devices in a mesh: ex: 16 (over z, y, core), hid: 2 (over x).
Axes of the slice: x: 2, y: 2, z: 4, core: 2. Of those that a mesh axis runs over, the one named last changes fastest.
Arguments:
- activations: bfloat16 [64, 192, 14336], P('ex', None, 'hid'), may hold values from -6 to 6
- out_grads: bfloat16 [64, 192, 4096], P('ex', None, 'hid'), may hold values from -6 to 6
- token_mask: int32 [64, 192], P('ex'), may hold values from 0 to 1, as said below
- proj_in: bfloat16 [14336, 64], P('hid'), may hold values from -0.046875 to 0.046875
- proj_out: bfloat16 [4096, 64], P('hid'), may hold values from -0.09375 to 0.09375
- inv_input: float32 [64, 64], replicated, as said below
- inv_output: float32 [64, 64], replicated, as said below
- query_feats: bfloat16 [1024, 4096], P('ex', 'hid'), may hold values from -6 to 6
Outputs:
- scores: float32 [1024, 64], P('ex', 'hid')
The draws below stay inside these ranges and needn't reach their ends.
Inputs may be any that keep to these rules, and one draw needn't show every extreme that they name: `token_mask`: each row is 48 or more ones followed by zeros; some row is all ones. `inv_input`: symmetric. `inv_output`: symmetric.
All inputs are finite; a program needn't handle non-finite values.
Results may differ from the reference program's by a relative error of at most 0.0041.
Values may be sent and summed in bfloat16 or wider, within the bound.
No kernel may reach another device: no remote copies, remote signals or barrier semaphores. Data moves between devices by JAX's collectives and lax.ppermute only.
A program may use at most 64 MiB of HBM per device.

```python
import math
import jax
import jax.numpy as jnp
from jax import lax

D = 4096
FF = 14336
RANK = 64
LEN = 192
TRAIN = 64
QUERIES = 1024
FEAT = 4096


def symmetric_factor(key):
    key_diag, key_off = jax.random.split(key)
    diag_vals = 1.0 + jax.random.uniform(key_diag, (RANK,), jnp.float32)
    noise = jax.random.normal(key_off, (RANK, RANK), jnp.float32)
    sym_noise = (noise + noise.T) * (0.4 / math.sqrt(2.0 * RANK))
    eye_mat = jnp.eye(RANK, dtype=jnp.float32)
    return sym_noise * (1.0 - eye_mat) + eye_mat * diag_vals[None, :]


def draw_inv_input(key, part):
    return symmetric_factor(jax.random.fold_in(key, 11))


def draw_inv_output(key, part):
    return symmetric_factor(jax.random.fold_in(key, 23))


def draw_token_mask(key, part):
    key_len, key_full = jax.random.split(jax.random.fold_in(key, 5))
    lengths = jax.random.randint(key_len, (TRAIN,), LEN // 4, LEN + 1)
    full_pick = jax.random.randint(key_full, (TRAIN,), 0, 4)
    lengths = jnp.where(full_pick == 0, LEN, lengths)
    lengths = lengths.at[0].set(LEN)
    positions = jnp.arange(LEN, dtype=jnp.int32)
    return (positions[None, :] < lengths[:, None]).astype(jnp.int32)


def block_levels(own_key, dims, shards, low, top_value):
    level, own = 1.0, jax.random.fold_in(own_key, 6)
    for axis_at, shards_of in shards:
        draws = jnp.exp(jax.random.uniform(jax.random.fold_in(own, axis_at), (shards_of,), jnp.float32, low / len(shards), top_value / len(shards)))
        level = level * jnp.repeat(draws, dims[axis_at] // shards_of).reshape([-1 if axis == axis_at else 1 for axis in range(len(dims))])
    return level


def gaussian(key, extent, deviation, reach, cuts=(), kind=jnp.bfloat16):
    values = deviation * jax.random.normal(key, extent, jnp.float32)
    if cuts:
        values = values * block_levels(key, extent, cuts, -0.22, 0.18)
    return jnp.clip(values, -reach, reach).astype(kind)


def setup_inputs(seed: int = 0) -> dict:
    arg_keys = jax.random.split(jax.random.key(seed), 9)
    return {
        "activations": gaussian(arg_keys[0], (TRAIN, LEN, FF), 1.0, 6.0, ((0, 16), (2, 2))),
        "out_grads": gaussian(arg_keys[1], (TRAIN, LEN, D), 1.0, 6.0, ((0, 16), (2, 2))),
        "token_mask": draw_token_mask(jax.random.fold_in(arg_keys[8], 71), 0),
        "proj_in": gaussian(arg_keys[3], (FF, RANK), FF ** -0.5, 0.046875, ((0, 2),)),
        "proj_out": gaussian(arg_keys[4], (D, RANK), D ** -0.5, 0.09375, ((0, 2),)),
        "inv_input": draw_inv_input(jax.random.fold_in(arg_keys[8], 71), 0),
        "inv_output": draw_inv_output(jax.random.fold_in(arg_keys[8], 71), 0),
        "query_feats": gaussian(arg_keys[7], (QUERIES, FEAT), 1.0, 6.0, ((0, 16), (1, 2))),
    }


def reference(activations, out_grads, token_mask, proj_in, proj_out, inv_input, inv_output, query_feats):
    in_side = jnp.dot(activations.reshape(TRAIN * LEN, FF), proj_in, preferred_element_type=jnp.float32)
    in_pre = jnp.dot(in_side, inv_input, precision=lax.Precision.HIGHEST)
    out_side = jnp.dot(out_grads.reshape(TRAIN * LEN, D), proj_out, preferred_element_type=jnp.float32)
    weights = token_mask.astype(jnp.float32)
    counted = jnp.sum(weights, axis=1)
    masked = in_pre.reshape(TRAIN, LEN, RANK) * weights[:, :, None]
    outer = jnp.einsum("slr,slq->srq", masked, out_side.reshape(TRAIN, LEN, RANK), precision=lax.Precision.HIGHEST)
    train_feats = (outer / counted[:, None, None]).astype(jnp.bfloat16).reshape(TRAIN, FEAT)
    queries = query_feats.reshape(QUERIES, RANK, RANK).astype(jnp.float32)
    query_pre = jnp.einsum("qij,jk->qik", queries, inv_output, precision=lax.Precision.HIGHEST)
    query_pre = query_pre.astype(jnp.bfloat16).reshape(QUERIES, FEAT)
    return jnp.dot(query_pre, train_feats.T, preferred_element_type=jnp.float32)
```

```python
import functools

import jax
import jax.numpy as jnp
from jax import lax
from jax.experimental import pallas as pl
from jax.experimental.pallas import tpu as pltpu
from jax.sharding import PartitionSpec as P

F32 = jnp.float32
BF16 = jnp.bfloat16
NT = (((1,), (1,)), ((), ()))
TN = (((0,), (0,)), ((), ()))
VMEM = pl.BlockSpec(memory_space=pltpu.VMEM)
ANY = pl.BlockSpec(memory_space=pl.ANY)
HIGH = lax.Precision.HIGHEST


def params(mib):
    return pltpu.CompilerParams(vmem_limit_bytes=mib << 20)


def project_kernel(chunks, x_hbm, w_ref, *rest):
    out_ref = rest[0]
    sent_ref = rest[1] if len(rest) == 4 else None
    buf, sems = rest[-2:]
    rows = x_hbm.shape[0]
    step = rows // chunks
    copies = [
        pltpu.make_async_copy(
            x_hbm.at[pl.ds(c * step, step)], buf.at[pl.ds(c * step, step)], sems.at[c]
        )
        for c in range(chunks)
    ]
    for copy in copies:
        copy.start()
    half = rows // 2
    rank = w_ref.shape[0]
    for c in range(chunks):
        copies[c].wait()
        part = lax.dot_general(
            buf[pl.ds(c * step, step), :], w_ref[...], NT, preferred_element_type=F32
        )
        row, lane = (c * step) % half, (c * step) // half * rank
        out_ref[pl.ds(row, step), pl.ds(lane, rank)] = part
    if sent_ref is not None:
        sent_ref[...] = out_ref[...].astype(BF16)


def project(x, w_t, chunks, send, mib):
    rows, depth = x.shape
    rank = w_t.shape[0]
    shape = (rows // 2, 2 * rank)
    outs = [jax.ShapeDtypeStruct(shape, F32)]
    if send:
        outs.append(jax.ShapeDtypeStruct(shape, BF16))
    return pl.pallas_call(
        functools.partial(project_kernel, chunks),
        out_shape=outs,
        in_specs=[ANY, VMEM],
        out_specs=[VMEM] * len(outs),
        scratch_shapes=[
            pltpu.VMEM((rows, depth), BF16),
            pltpu.SemaphoreType.DMA((chunks,)),
        ],
        compiler_params=params(mib),
        cost_estimate=pl.CostEstimate(
            flops=2 * rows * depth * rank, bytes_accessed=2 * rows * depth, transcendentals=0
        ),
    )(x, w_t)


def outer_kernel(
    length, in_ref, own_ref, got_ref, mask_ref, inv_ref, part_ref, sent_ref, rows_ref, pairs_ref
):
    rank = inv_ref.shape[0]
    seqs = mask_ref.shape[0]
    counts = jnp.sum(mask_ref[...].astype(F32), axis=1, keepdims=True)
    lane = lax.broadcasted_iota(jnp.int32, (length, 2 * rank), 1)
    token = lax.broadcasted_iota(jnp.int32, (length, 2 * rank), 0).astype(F32)
    grams = [None] * seqs
    for pair in range(seqs // 2):
        rows = pl.ds(pair * length, length)
        low, high = counts[pair : pair + 1, :], counts[pair + seqs // 2 : pair + seqs // 2 + 1, :]
        real = token < jnp.where(lane < rank, low, high)
        inside = jnp.where(real, in_ref[rows, :], 0.0)
        outside = own_ref[rows, :] + got_ref[rows, :].astype(F32)
        both = lax.dot_general(
            inside, outside, TN, precision=HIGH, preferred_element_type=F32
        )
        grams[pair] = both[:rank, :rank] / low
        grams[pair + seqs // 2] = both[rank:, rank:] / high
    gram = jnp.concatenate(grams, axis=1)
    pre = lax.dot_general(inv_ref[...], gram, TN, precision=HIGH, preferred_element_type=F32)
    half = rank // 2
    for s in range(seqs):
        rows_ref[...] = pre[:, s * rank : (s + 1) * rank]
        pairs_ref[pl.ds(s * half, half), :] = jnp.concatenate(
            [rows_ref[pl.ds(0, half, stride=2), :], rows_ref[pl.ds(1, half, stride=2), :]], axis=1
        )
    for b in range(half):
        row = pairs_ref[pl.ds(b, seqs, stride=half), :]
        part_ref[:, pl.ds(b * 2 * rank, 2 * rank)] = row
    sent_ref[...] = part_ref[...].astype(BF16)


def outer(in_part, out_own, out_got, token_mask, inv_input):
    seqs, length = token_mask.shape
    rank = inv_input.shape[0]
    shape = (seqs, rank * rank)
    return pl.pallas_call(
        functools.partial(outer_kernel, length),
        out_shape=[jax.ShapeDtypeStruct(shape, F32), jax.ShapeDtypeStruct(shape, BF16)],
        in_specs=[VMEM] * 5,
        out_specs=[VMEM] * 2,
        scratch_shapes=[
            pltpu.VMEM((rank, rank), F32),
            pltpu.VMEM((seqs * rank // 2, 2 * rank), F32),
        ],
        compiler_params=params(16),
    )(in_part, out_own, out_got, token_mask, inv_input)


def query_kernel(query_ref, inv_ref, pre_ref):
    rank = inv_ref.shape[0]
    zero = jnp.zeros((rank, rank), F32)
    inv = inv_ref[...]
    block = jnp.concatenate(
        [jnp.concatenate([inv, zero], axis=1), jnp.concatenate([zero, inv], axis=1)], axis=0
    )
    top = block.astype(BF16)
    rest = block - top.astype(F32)
    middle = rest.astype(BF16)
    last = (rest - middle.astype(F32)).astype(BF16)
    for b in range(query_ref.shape[1] // (2 * rank)):
        lanes = pl.ds(b * 2 * rank, 2 * rank)
        query = query_ref[:, lanes]
        total = jnp.dot(query, last, preferred_element_type=F32)
        total += jnp.dot(query, middle, preferred_element_type=F32)
        total += jnp.dot(query, top, preferred_element_type=F32)
        pre_ref[:, lanes] = total.astype(BF16)


def precondition_queries(query_feats, inv_output):
    return pl.pallas_call(
        query_kernel,
        out_shape=jax.ShapeDtypeStruct(query_feats.shape, BF16),
        in_specs=[VMEM] * 2,
        out_specs=VMEM,
        compiler_params=params(16),
    )(query_feats, inv_output)


def score_kernel(place_ref, low_ref, high_ref, *rest):
    *pieces, out_ref, feats_ref = rest
    seqs = pieces[0].shape[0]
    for k, piece in enumerate(pieces):
        feats_ref[pl.ds(k * seqs, seqs), :] = piece[...].astype(F32)
    half = low_ref.shape[1]
    feats = feats_ref[...].astype(BF16)
    scores = lax.dot_general(feats[:, :half], low_ref[...], NT, preferred_element_type=F32)
    scores += lax.dot_general(feats[:, half:], high_ref[...], NT, preferred_element_type=F32)
    rows = scores.shape[0]
    at = lax.broadcasted_iota(jnp.int32, scores.shape, 0)
    place = place_ref[0]
    size = seqs
    while size < rows:
        swapped = jnp.where(
            (at & size) == 0, pltpu.roll(scores, rows - size, 0), pltpu.roll(scores, size, 0)
        )
        bit = (place & (size // seqs)) != 0
        scores = jnp.where(bit, swapped, scores)
        size *= 2
    out_ref[...] = scores


def score(place, low, high, pieces):
    seqs, feats = pieces[0].shape
    rows = seqs * len(pieces)
    return pl.pallas_call(
        score_kernel,
        out_shape=jax.ShapeDtypeStruct((rows, low.shape[0]), F32),
        in_specs=[pl.BlockSpec(memory_space=pltpu.SMEM)] + [VMEM] * (2 + len(pieces)),
        out_specs=VMEM,
        scratch_shapes=[pltpu.VMEM((rows, feats), F32)],
        compiler_params=params(16),
    )(place, low, high, *pieces)


def local_pair(
    activations, out_grads, token_mask, proj_in, proj_out, inv_input, inv_output, query_feats
):
    seqs, length, depth = activations.shape
    ex_size = lax.axis_size("ex")
    ex = lax.axis_index("ex")
    hid = lax.axis_index("hid")
    half = ex_size // 2
    swap_hid = [(0, 1), (1, 0)]

    out_own, out_sent = project(
        out_grads.reshape(seqs * length, -1), proj_out.T, 4, True, 16
    )
    out_got = lax.ppermute(out_sent, "hid", swap_hid)
    (in_part,) = project(activations.reshape(seqs * length, depth), proj_in.T, 8, False, 32)
    part, sent = outer(in_part, out_own, out_got, token_mask, inv_input)

    around, across = [], []
    for e in range(half):
        a, b, c, d = 2 * e + 1, 2 * e, 2 * (e + half), 2 * (e + half) + 1
        around += [(a, b), (b, c), (c, d), (d, a)]
        across += [(a, c), (c, a), (b, d), (d, b)]
    axes = ("ex", "hid")
    first = lax.ppermute(sent, axes, around)
    second = lax.ppermute(sent, axes, across)
    home = (ex // half) == hid
    mine = (
        first.astype(F32) + jnp.where(home, part, second.astype(F32))
    ).astype(BF16)

    query_own = precondition_queries(query_feats, inv_output)
    query_got = lax.ppermute(query_own, "hid", swap_hid)
    low = jnp.where(hid == 0, query_own, query_got)
    high = jnp.where(hid == 0, query_got, query_own)

    pieces = [mine]
    far = [k for k in range(2, half, 2)]
    pieces = {0: mine}
    for k in sorted(far, key=lambda k: -k):
        pieces[k] = lax.ppermute(mine, "ex", [(i, i ^ k) for i in range(ex_size)])
    for k in list(pieces):
        pieces[k ^ 1] = lax.ppermute(pieces[k], "ex", [(i, i ^ 1) for i in range(ex_size)])
    place = (ex % half).astype(jnp.int32).reshape(1)
    scores = score(place, low, high, [pieces[k] for k in range(half)])
    return scores.T


def local_any(
    activations, out_grads, token_mask, proj_in, proj_out, inv_input, inv_output, query_feats
):
    seq_count, length, unit_local = activations.shape
    rank_width = proj_in.shape[1]
    hid_size = lax.axis_size("hid")
    row_block = rank_width // hid_size
    my_index = lax.axis_index("hid")
    in_part = jnp.dot(
        activations.reshape(seq_count * length, unit_local),
        proj_in,
        preferred_element_type=F32,
    )
    in_part = jnp.dot(in_part, inv_input, precision=HIGH)
    out_part = jnp.dot(
        out_grads.reshape(seq_count * length, out_grads.shape[2]),
        proj_out,
        preferred_element_type=F32,
    )
    token_weight = token_mask.astype(F32)
    tok_count = jnp.sum(token_weight, axis=1)
    in_full, out_full = lax.psum((in_part, out_part), "hid")
    in_mine = lax.dynamic_slice_in_dim(in_full, my_index * row_block, row_block, 1)
    masked = in_mine.reshape(seq_count, length, row_block) * token_weight[:, :, None]
    outer_sum = jnp.einsum(
        "slr,slq->srq",
        masked,
        out_full.reshape(seq_count, length, rank_width),
        precision=HIGH,
    )
    train_feats = (
        (outer_sum / tok_count[:, None, None])
        .astype(BF16)
        .reshape(seq_count, row_block * rank_width)
    )
    query_count = query_feats.shape[0]
    queries = query_feats.reshape(query_count, row_block, rank_width).astype(F32)
    query_pre = jnp.einsum("qij,jk->qik", queries, inv_output, precision=HIGH)
    query_pre = query_pre.astype(BF16).reshape(query_count, row_block * rank_width)
    partial_value = jnp.einsum(
        "qk,tk->qt",
        query_pre,
        lax.all_gather(train_feats, "ex", axis=0, tiled=True),
        preferred_element_type=F32,
    )
    return lax.psum_scatter(partial_value, "hid", scatter_dimension=1, tiled=True)


def solution(mesh):
    ex_size, hid_size = mesh.shape["ex"], mesh.shape["hid"]
    paired = hid_size == 2 and ex_size >= 4 and ex_size & (ex_size - 1) == 0
    return jax.shard_map(
        local_pair if paired else local_any,
        mesh=mesh,
        in_specs=(
            P("ex", None, "hid"),
            P("ex", None, "hid"),
            P("ex", None),
            P("hid", None),
            P("hid", None),
            P(),
            P(),
            P("ex", "hid"),
        ),
        out_specs=P("ex", "hid"),
        check_vma=False,
    )
```

```python
import functools

import jax
import jax.numpy as jnp
from jax import lax
from jax.experimental import pallas as pl
from jax.experimental.pallas import tpu as pltpu
from jax.sharding import PartitionSpec as P

F32 = jnp.float32
BF16 = jnp.bfloat16
NT = (((1,), (1,)), ((), ()))
TN = (((0,), (0,)), ((), ()))
VMEM = pl.BlockSpec(memory_space=pltpu.VMEM)
HBM = pl.BlockSpec(memory_space=pltpu.HBM)
HIGH = lax.Precision.HIGHEST


def params(mib):
    return pltpu.CompilerParams(vmem_limit_bytes=mib << 20)


def hbm(x):
    return pltpu.with_memory_space_constraint(x, pltpu.HBM)


def out_kernel(chunks, x_hbm, w_hbm, out_ref, sent_ref, x_ref, wide_ref, tall_ref, sems):
    rows = x_hbm.shape[0]
    step = rows // chunks
    weights = pltpu.make_async_copy(w_hbm, wide_ref, sems.at[chunks])
    weights.start()
    copies = [
        pltpu.make_async_copy(
            x_hbm.at[pl.ds(c * step, step)], x_ref.at[pl.ds(c * step, step)], sems.at[c]
        )
        for c in range(chunks)
    ]
    for copy in copies:
        copy.start()
    weights.wait()
    tall_ref[...] = wide_ref[...].T
    half = rows // 2
    rank = w_hbm.shape[0]
    for side in range(2):
        for copy in copies[side * chunks // 2 : (side + 1) * chunks // 2]:
            copy.wait()
        part = jnp.dot(
            x_ref[pl.ds(side * half, half), :], tall_ref[...], preferred_element_type=F32
        )
        out_ref[:, pl.ds(side * rank, rank)] = part
        sent_ref[:, pl.ds(side * rank, rank)] = part.astype(BF16)


def project_out(x, w_t, chunks):
    rows, depth = x.shape
    rank = w_t.shape[0]
    shape = (rows // 2, 2 * rank)
    return pl.pallas_call(
        functools.partial(out_kernel, chunks),
        out_shape=[jax.ShapeDtypeStruct(shape, F32), jax.ShapeDtypeStruct(shape, BF16)],
        in_specs=[HBM, HBM],
        out_specs=[VMEM] * 2,
        scratch_shapes=[
            pltpu.VMEM((rows, depth), BF16),
            pltpu.VMEM((rank, depth), BF16),
            pltpu.VMEM((depth, rank), BF16),
            pltpu.SemaphoreType.DMA((chunks + 1,)),
        ],
        compiler_params=params(16),
        cost_estimate=pl.CostEstimate(
            flops=60 * rows * depth * rank, bytes_accessed=60 * rows * depth, transcendentals=0
        ),
    )(hbm(x), hbm(w_t))


def in_kernel(x_ref, w_ref, out_ref, tall_ref):
    half = x_ref.shape[0] // 2
    rank = w_ref.shape[0]
    tall_ref[...] = w_ref[...].T
    for side in range(2):
        part = jnp.dot(
            x_ref[pl.ds(side * half, half), :], tall_ref[...], preferred_element_type=F32
        )
        out_ref[:, pl.ds(side * rank, rank)] = part


def project_in(x, w_t):
    rows, depth = x.shape
    rank = w_t.shape[0]
    return pl.pallas_call(
        in_kernel,
        out_shape=jax.ShapeDtypeStruct((rows // 2, 2 * rank), F32),
        in_specs=[VMEM, VMEM],
        out_specs=VMEM,
        scratch_shapes=[pltpu.VMEM((depth, rank), BF16)],
        compiler_params=params(16),
        cost_estimate=pl.CostEstimate(
            flops=2 * rows * depth * rank, bytes_accessed=2 * rows * depth, transcendentals=0
        ),
    )(x, w_t)


def outer_kernel(
    length, in_ref, own_ref, got_ref, mask_ref, inv_ref, part_ref, sent_ref, rows_ref, pairs_ref
):
    rank = inv_ref.shape[0]
    seqs = mask_ref.shape[0]
    counts = jnp.sum(mask_ref[...].astype(F32), axis=1, keepdims=True)
    lane = lax.broadcasted_iota(jnp.int32, (length, 2 * rank), 1)
    token = lax.broadcasted_iota(jnp.int32, (length, 2 * rank), 0).astype(F32)
    grams = [None] * seqs
    for pair in range(seqs // 2):
        rows = pl.ds(pair * length, length)
        low, high = counts[pair : pair + 1, :], counts[pair + seqs // 2 : pair + seqs // 2 + 1, :]
        real = token < jnp.where(lane < rank, low, high)
        inside = jnp.where(real, in_ref[rows, :], 0.0)
        outside = own_ref[rows, :] + got_ref[rows, :].astype(F32)
        both = lax.dot_general(
            inside, outside, TN, precision=HIGH, preferred_element_type=F32
        )
        grams[pair] = both[:rank, :rank] / low
        grams[pair + seqs // 2] = both[rank:, rank:] / high
    gram = jnp.concatenate(grams, axis=1)
    pre = lax.dot_general(inv_ref[...], gram, TN, precision=HIGH, preferred_element_type=F32)
    half = rank // 2
    for s in range(seqs):
        rows_ref[...] = pre[:, s * rank : (s + 1) * rank]
        pairs_ref[pl.ds(s * half, half), :] = jnp.concatenate(
            [rows_ref[pl.ds(0, half, stride=2), :], rows_ref[pl.ds(1, half, stride=2), :]], axis=1
        )
    for b in range(half):
        row = pairs_ref[pl.ds(b, seqs, stride=half), :]
        part_ref[:, pl.ds(b * 2 * rank, 2 * rank)] = row
    sent_ref[...] = part_ref[...].astype(BF16)


def outer(in_part, out_own, out_got, token_mask, inv_input):
    seqs, length = token_mask.shape
    rank = inv_input.shape[0]
    shape = (seqs, rank * rank)
    return pl.pallas_call(
        functools.partial(outer_kernel, length),
        out_shape=[jax.ShapeDtypeStruct(shape, F32), jax.ShapeDtypeStruct(shape, BF16)],
        in_specs=[VMEM] * 5,
        out_specs=[VMEM] * 2,
        scratch_shapes=[
            pltpu.VMEM((rank, rank), F32),
            pltpu.VMEM((seqs * rank // 2, 2 * rank), F32),
        ],
        compiler_params=params(16),
    )(in_part, out_own, out_got, token_mask, inv_input)


def query_kernel(query_ref, inv_ref, pre_ref):
    rank = inv_ref.shape[0]
    zero = jnp.zeros((rank, rank), F32)
    inv = inv_ref[...]
    block = jnp.concatenate(
        [jnp.concatenate([inv, zero], axis=1), jnp.concatenate([zero, inv], axis=1)], axis=0
    )
    top = block.astype(BF16)
    rest = block - top.astype(F32)
    middle = rest.astype(BF16)
    last = (rest - middle.astype(F32)).astype(BF16)
    for b in range(query_ref.shape[1] // (2 * rank)):
        lanes = pl.ds(b * 2 * rank, 2 * rank)
        query = query_ref[:, lanes]
        total = jnp.dot(query, last, preferred_element_type=F32)
        total += jnp.dot(query, middle, preferred_element_type=F32)
        total += jnp.dot(query, top, preferred_element_type=F32)
        pre_ref[:, lanes] = total.astype(BF16)


def precondition_queries(query_feats, inv_output):
    return pl.pallas_call(
        query_kernel,
        out_shape=jax.ShapeDtypeStruct(query_feats.shape, BF16),
        in_specs=[VMEM] * 2,
        out_specs=VMEM,
        compiler_params=params(16),
    )(query_feats, inv_output)


def score_kernel(place_ref, low_ref, high_ref, *rest):
    *pieces, out_ref, feats_ref = rest
    seqs = pieces[0].shape[0]
    for k, piece in enumerate(pieces):
        feats_ref[pl.ds(k * seqs, seqs), :] = piece[...].astype(F32)
    half = low_ref.shape[1]
    feats = feats_ref[...].astype(BF16)
    scores = lax.dot_general(feats[:, :half], low_ref[...], NT, preferred_element_type=F32)
    scores += lax.dot_general(feats[:, half:], high_ref[...], NT, preferred_element_type=F32)
    rows = scores.shape[0]
    at = lax.broadcasted_iota(jnp.int32, scores.shape, 0)
    place = place_ref[0]
    size = seqs
    while size < rows:
        swapped = jnp.where(
            (at & size) == 0, pltpu.roll(scores, rows - size, 0), pltpu.roll(scores, size, 0)
        )
        bit = (place & (size // seqs)) != 0
        scores = jnp.where(bit, swapped, scores)
        size *= 2
    out_ref[...] = scores


def score(place, low, high, pieces):
    seqs, feats = pieces[0].shape
    rows = seqs * len(pieces)
    return pl.pallas_call(
        score_kernel,
        out_shape=jax.ShapeDtypeStruct((rows, low.shape[0]), F32),
        in_specs=[pl.BlockSpec(memory_space=pltpu.SMEM)] + [VMEM] * (2 + len(pieces)),
        out_specs=VMEM,
        scratch_shapes=[pltpu.VMEM((rows, feats), F32)],
        compiler_params=params(16),
    )(place, low, high, *pieces)


def local_pair(
    activations, out_grads, token_mask, proj_in, proj_out, inv_input, inv_output, query_feats
):
    seqs, length, depth = activations.shape
    ex_size = lax.axis_size("ex")
    ex = lax.axis_index("ex")
    hid = lax.axis_index("hid")
    half = ex_size // 2
    swap_hid = [(0, 1), (1, 0)]

    out_own, out_sent = project_out(out_grads.reshape(seqs * length, -1), proj_out.T, 4)
    out_got = lax.ppermute(out_sent, "hid", swap_hid)
    in_part = project_in(activations.reshape(seqs * length, depth), proj_in.T)
    part, sent = outer(in_part, out_own, out_got, token_mask, inv_input)

    around, across = [], []
    for e in range(half):
        a, b, c, d = 2 * e + 1, 2 * e, 2 * (e + half), 2 * (e + half) + 1
        around += [(a, b), (b, c), (c, d), (d, a)]
        across += [(a, c), (c, a), (b, d), (d, b)]
    axes = ("ex", "hid")
    first = lax.ppermute(sent, axes, around)
    second = lax.ppermute(sent, axes, across)
    home = (ex // half) == hid
    mine = (
        first.astype(F32) + jnp.where(home, part, second.astype(F32))
    ).astype(BF16)

    query_own = precondition_queries(query_feats, inv_output)
    query_got = lax.ppermute(query_own, "hid", swap_hid)
    low = jnp.where(hid == 0, query_own, query_got)
    high = jnp.where(hid == 0, query_got, query_own)

    pieces = [mine]
    far = [k for k in range(2, half, 2)]
    pieces = {0: mine}
    for k in sorted(far, key=lambda k: -k):
        pieces[k] = lax.ppermute(mine, "ex", [(i, i ^ k) for i in range(ex_size)])
    for k in list(pieces):
        pieces[k ^ 1] = lax.ppermute(pieces[k], "ex", [(i, i ^ 1) for i in range(ex_size)])
    place = (ex % half).astype(jnp.int32).reshape(1)
    scores = score(place, low, high, [pieces[k] for k in range(half)])
    return scores.T


def local_any(
    activations, out_grads, token_mask, proj_in, proj_out, inv_input, inv_output, query_feats
):
    seq_count, length, unit_local = activations.shape
    rank_width = proj_in.shape[1]
    hid_size = lax.axis_size("hid")
    row_block = rank_width // hid_size
    my_index = lax.axis_index("hid")
    in_part = jnp.dot(
        activations.reshape(seq_count * length, unit_local),
        proj_in,
        preferred_element_type=F32,
    )
    in_part = jnp.dot(in_part, inv_input, precision=HIGH)
    out_part = jnp.dot(
        out_grads.reshape(seq_count * length, out_grads.shape[2]),
        proj_out,
        preferred_element_type=F32,
    )
    token_weight = token_mask.astype(F32)
    tok_count = jnp.sum(token_weight, axis=1)
    in_full, out_full = lax.psum((in_part, out_part), "hid")
    in_mine = lax.dynamic_slice_in_dim(in_full, my_index * row_block, row_block, 1)
    masked = in_mine.reshape(seq_count, length, row_block) * token_weight[:, :, None]
    outer_sum = jnp.einsum(
        "slr,slq->srq",
        masked,
        out_full.reshape(seq_count, length, rank_width),
        precision=HIGH,
    )
    train_feats = (
        (outer_sum / tok_count[:, None, None])
        .astype(BF16)
        .reshape(seq_count, row_block * rank_width)
    )
    query_count = query_feats.shape[0]
    queries = query_feats.reshape(query_count, row_block, rank_width).astype(F32)
    query_pre = jnp.einsum("qij,jk->qik", queries, inv_output, precision=HIGH)
    query_pre = query_pre.astype(BF16).reshape(query_count, row_block * rank_width)
    partial_value = jnp.einsum(
        "qk,tk->qt",
        query_pre,
        lax.all_gather(train_feats, "ex", axis=0, tiled=True),
        preferred_element_type=F32,
    )
    return lax.psum_scatter(partial_value, "hid", scatter_dimension=1, tiled=True)


def solution(mesh):
    ex_size, hid_size = mesh.shape["ex"], mesh.shape["hid"]
    paired = hid_size == 2 and ex_size >= 4 and ex_size & (ex_size - 1) == 0
    return jax.shard_map(
        local_pair if paired else local_any,
        mesh=mesh,
        in_specs=(
            P("ex", None, "hid"),
            P("ex", None, "hid"),
            P("ex", None),
            P("hid", None),
            P("hid", None),
            P(),
            P(),
            P("ex", "hid"),
        ),
        out_specs=P("ex", "hid"),
        check_vma=False,
    )
```

```python
import functools

import jax
import jax.numpy as jnp
from jax import lax
from jax.experimental import pallas as pl
from jax.experimental.pallas import tpu as pltpu
from jax.sharding import PartitionSpec as P

F32 = jnp.float32
BF16 = jnp.bfloat16
NT = (((1,), (1,)), ((), ()))
TN = (((0,), (0,)), ((), ()))
VMEM = pl.BlockSpec(memory_space=pltpu.VMEM)
HBM = pl.BlockSpec(memory_space=pltpu.HBM)
HIGH = lax.Precision.HIGHEST


def params(mib):
    return pltpu.CompilerParams(vmem_limit_bytes=mib << 20)


def hbm(x):
    return pltpu.with_memory_space_constraint(x, pltpu.HBM)


def out_kernel(chunks, x_hbm, w_hbm, out_ref, sent_ref, x_ref, wide_ref, tall_ref, sems):
    rows = x_hbm.shape[0]
    step = rows // chunks
    weights = pltpu.make_async_copy(w_hbm, wide_ref, sems.at[chunks])
    weights.start()
    copies = [
        pltpu.make_async_copy(
            x_hbm.at[pl.ds(c * step, step)], x_ref.at[pl.ds(c * step, step)], sems.at[c]
        )
        for c in range(chunks)
    ]
    for copy in copies:
        copy.start()
    weights.wait()
    tall_ref[...] = wide_ref[...].T
    half = rows // 2
    rank = w_hbm.shape[0]
    for side in range(2):
        for copy in copies[side * chunks // 2 : (side + 1) * chunks // 2]:
            copy.wait()
        part = jnp.dot(
            x_ref[pl.ds(side * half, half), :], tall_ref[...], preferred_element_type=F32
        )
        out_ref[:, pl.ds(side * rank, rank)] = part
        sent_ref[:, pl.ds(side * rank, rank)] = part.astype(BF16)


def project_out(x, w_t, chunks):
    rows, depth = x.shape
    rank = w_t.shape[0]
    shape = (rows // 2, 2 * rank)
    return pl.pallas_call(
        functools.partial(out_kernel, chunks),
        out_shape=[jax.ShapeDtypeStruct(shape, F32), jax.ShapeDtypeStruct(shape, BF16)],
        in_specs=[HBM, HBM],
        out_specs=[VMEM] * 2,
        scratch_shapes=[
            pltpu.VMEM((rows, depth), BF16),
            pltpu.VMEM((rank, depth), BF16),
            pltpu.VMEM((depth, rank), BF16),
            pltpu.SemaphoreType.DMA((chunks + 1,)),
        ],
        compiler_params=params(16),
        cost_estimate=pl.CostEstimate(
            flops=60 * rows * depth * rank, bytes_accessed=60 * rows * depth, transcendentals=0
        ),
    )(hbm(x), hbm(w_t))


def in_kernel(x_ref, w_ref, out_ref, tall_ref):
    half = x_ref.shape[0] // 2
    rank = w_ref.shape[0]
    tall_ref[...] = w_ref[...].T
    for side in range(2):
        part = jnp.dot(
            x_ref[pl.ds(side * half, half), :], tall_ref[...], preferred_element_type=F32
        )
        out_ref[:, pl.ds(side * rank, rank)] = part


def project_in(x, w_t):
    rows, depth = x.shape
    rank = w_t.shape[0]
    return pl.pallas_call(
        in_kernel,
        out_shape=jax.ShapeDtypeStruct((rows // 2, 2 * rank), F32),
        in_specs=[VMEM, VMEM],
        out_specs=VMEM,
        scratch_shapes=[pltpu.VMEM((depth, rank), BF16)],
        compiler_params=params(16),
        cost_estimate=pl.CostEstimate(
            flops=2 * rows * depth * rank, bytes_accessed=2 * rows * depth, transcendentals=0
        ),
    )(x, w_t)


def outer_kernel(
    length, in_ref, own_ref, got_ref, mask_ref, inv_ref, part_ref, sent_ref, rows_ref, pairs_ref
):
    rank = inv_ref.shape[0]
    seqs = mask_ref.shape[0]
    counts = jnp.sum(mask_ref[...].astype(F32), axis=1, keepdims=True)
    lane = lax.broadcasted_iota(jnp.int32, (length, 2 * rank), 1)
    token = lax.broadcasted_iota(jnp.int32, (length, 2 * rank), 0).astype(F32)
    grams = [None] * seqs
    for pair in range(seqs // 2):
        rows = pl.ds(pair * length, length)
        low, high = counts[pair : pair + 1, :], counts[pair + seqs // 2 : pair + seqs // 2 + 1, :]
        real = token < jnp.where(lane < rank, low, high)
        inside = jnp.where(real, in_ref[rows, :], 0.0)
        outside = own_ref[rows, :] + got_ref[rows, :].astype(F32)
        both = lax.dot_general(
            inside, outside, TN, precision=HIGH, preferred_element_type=F32
        )
        grams[pair] = both[:rank, :rank] / low
        grams[pair + seqs // 2] = both[rank:, rank:] / high
    gram = jnp.concatenate(grams, axis=1)
    pre = lax.dot_general(inv_ref[...], gram, TN, precision=HIGH, preferred_element_type=F32)
    half = rank // 2
    for s in range(seqs):
        rows_ref[...] = pre[:, s * rank : (s + 1) * rank]
        pairs_ref[pl.ds(s * half, half), :] = jnp.concatenate(
            [rows_ref[pl.ds(0, half, stride=2), :], rows_ref[pl.ds(1, half, stride=2), :]], axis=1
        )
    for b in range(half):
        row = pairs_ref[pl.ds(b, seqs, stride=half), :]
        part_ref[:, pl.ds(b * 2 * rank, 2 * rank)] = row
    sent_ref[...] = part_ref[...].astype(BF16)


def outer(in_part, out_own, out_got, token_mask, inv_input):
    seqs, length = token_mask.shape
    rank = inv_input.shape[0]
    shape = (seqs, rank * rank)
    return pl.pallas_call(
        functools.partial(outer_kernel, length),
        out_shape=[jax.ShapeDtypeStruct(shape, F32), jax.ShapeDtypeStruct(shape, BF16)],
        in_specs=[VMEM] * 5,
        out_specs=[VMEM] * 2,
        scratch_shapes=[
            pltpu.VMEM((rank, rank), F32),
            pltpu.VMEM((seqs * rank // 2, 2 * rank), F32),
        ],
        compiler_params=params(16),
    )(in_part, out_own, out_got, token_mask, inv_input)


def query_kernel(query_ref, inv_ref, pre_ref):
    rank = inv_ref.shape[0]
    zero = jnp.zeros((rank, rank), F32)
    inv = inv_ref[...]
    block = jnp.concatenate(
        [jnp.concatenate([inv, zero], axis=1), jnp.concatenate([zero, inv], axis=1)], axis=0
    )
    top = block.astype(BF16)
    rest = block - top.astype(F32)
    middle = rest.astype(BF16)
    last = (rest - middle.astype(F32)).astype(BF16)
    for b in range(query_ref.shape[1] // (2 * rank)):
        lanes = pl.ds(b * 2 * rank, 2 * rank)
        query = query_ref[:, lanes]
        total = jnp.dot(query, last, preferred_element_type=F32)
        total += jnp.dot(query, middle, preferred_element_type=F32)
        total += jnp.dot(query, top, preferred_element_type=F32)
        pre_ref[:, lanes] = total.astype(BF16)


def precondition_queries(query_feats, inv_output):
    return pl.pallas_call(
        query_kernel,
        out_shape=jax.ShapeDtypeStruct(query_feats.shape, BF16),
        in_specs=[VMEM] * 2,
        out_specs=VMEM,
        compiler_params=params(16),
    )(query_feats, inv_output)


def score_kernel(place_ref, low_ref, high_ref, *rest):
    *pieces, out_ref, feats_ref = rest
    seqs = pieces[0].shape[0]
    for k, piece in enumerate(pieces):
        feats_ref[pl.ds(k * seqs, seqs), :] = piece[...].astype(F32)
    half = low_ref.shape[1]
    feats = feats_ref[...].astype(BF16)
    scores = lax.dot_general(low_ref[...], feats[:, :half], NT, preferred_element_type=F32)
    scores += lax.dot_general(high_ref[...], feats[:, half:], NT, preferred_element_type=F32)
    scores = scores.T
    rows = scores.shape[0]
    at = lax.broadcasted_iota(jnp.int32, scores.shape, 0)
    size = seqs
    while size < rows:
        swapped = jnp.where(
            (at & size) == 0, pltpu.roll(scores, rows - size, 0), pltpu.roll(scores, size, 0)
        )
        bit = (place_ref[...] & (size // seqs)) != 0
        scores = jnp.where(bit, swapped, scores)
        size *= 2
    out_ref[...] = scores


def score(place, low, high, pieces):
    seqs, feats = pieces[0].shape
    rows = seqs * len(pieces)
    return pl.pallas_call(
        score_kernel,
        out_shape=jax.ShapeDtypeStruct((rows, low.shape[0]), F32),
        in_specs=[VMEM] * (3 + len(pieces)),
        out_specs=VMEM,
        scratch_shapes=[pltpu.VMEM((rows, feats), F32)],
        compiler_params=params(16),
    )(place, low, high, *pieces)


def local_pair(
    activations, out_grads, token_mask, proj_in, proj_out, inv_input, inv_output, query_feats
):
    seqs, length, depth = activations.shape
    ex_size = lax.axis_size("ex")
    ex = lax.axis_index("ex")
    hid = lax.axis_index("hid")
    half = ex_size // 2
    swap_hid = [(0, 1), (1, 0)]

    out_own, out_sent = project_out(out_grads.reshape(seqs * length, -1), proj_out.T, 4)
    out_got = lax.ppermute(out_sent, "hid", swap_hid)
    in_part = project_in(activations.reshape(seqs * length, depth), proj_in.T)
    part, sent = outer(in_part, out_own, out_got, token_mask, inv_input)

    around, across = [], []
    for e in range(half):
        a, b, c, d = 2 * e + 1, 2 * e, 2 * (e + half), 2 * (e + half) + 1
        around += [(a, b), (b, c), (c, d), (d, a)]
        across += [(a, c), (c, a), (b, d), (d, b)]
    axes = ("ex", "hid")
    second = lax.ppermute(sent, axes, across)
    first = lax.ppermute(sent, axes, around)
    home = (ex // half) == hid
    mine = (
        jnp.where(home, part, second.astype(F32)) + first.astype(F32)
    ).astype(BF16)

    query_own = precondition_queries(query_feats, inv_output)
    query_got = lax.ppermute(query_own, "hid", swap_hid)
    low = jnp.where(hid == 0, query_own, query_got)
    high = jnp.where(hid == 0, query_got, query_own)

    pieces = [mine]
    far = [k for k in range(2, half, 2)]
    pieces = {0: mine}
    for k in sorted(far, key=lambda k: -k):
        pieces[k] = lax.ppermute(mine, "ex", [(i, i ^ k) for i in range(ex_size)])
    for k in list(pieces):
        pieces[k ^ 1] = lax.ppermute(pieces[k], "ex", [(i, i ^ 1) for i in range(ex_size)])
    place = jnp.full((seqs * half, query_feats.shape[0]), ex % half, jnp.int32)
    scores = score(place, low, high, [pieces[k] for k in range(half)])
    return scores.T


def local_any(
    activations, out_grads, token_mask, proj_in, proj_out, inv_input, inv_output, query_feats
):
    seq_count, length, unit_local = activations.shape
    rank_width = proj_in.shape[1]
    hid_size = lax.axis_size("hid")
    row_block = rank_width // hid_size
    my_index = lax.axis_index("hid")
    in_part = jnp.dot(
        activations.reshape(seq_count * length, unit_local),
        proj_in,
        preferred_element_type=F32,
    )
    in_part = jnp.dot(in_part, inv_input, precision=HIGH)
    out_part = jnp.dot(
        out_grads.reshape(seq_count * length, out_grads.shape[2]),
        proj_out,
        preferred_element_type=F32,
    )
    token_weight = token_mask.astype(F32)
    tok_count = jnp.sum(token_weight, axis=1)
    in_full, out_full = lax.psum((in_part, out_part), "hid")
    in_mine = lax.dynamic_slice_in_dim(in_full, my_index * row_block, row_block, 1)
    masked = in_mine.reshape(seq_count, length, row_block) * token_weight[:, :, None]
    outer_sum = jnp.einsum(
        "slr,slq->srq",
        masked,
        out_full.reshape(seq_count, length, rank_width),
        precision=HIGH,
    )
    train_feats = (
        (outer_sum / tok_count[:, None, None])
        .astype(BF16)
        .reshape(seq_count, row_block * rank_width)
    )
    query_count = query_feats.shape[0]
    queries = query_feats.reshape(query_count, row_block, rank_width).astype(F32)
    query_pre = jnp.einsum("qij,jk->qik", queries, inv_output, precision=HIGH)
    query_pre = query_pre.astype(BF16).reshape(query_count, row_block * rank_width)
    partial_value = jnp.einsum(
        "qk,tk->qt",
        query_pre,
        lax.all_gather(train_feats, "ex", axis=0, tiled=True),
        preferred_element_type=F32,
    )
    return lax.psum_scatter(partial_value, "hid", scatter_dimension=1, tiled=True)


def solution(mesh):
    ex_size, hid_size = mesh.shape["ex"], mesh.shape["hid"]
    paired = hid_size == 2 and ex_size >= 4 and ex_size & (ex_size - 1) == 0
    return jax.shard_map(
        local_pair if paired else local_any,
        mesh=mesh,
        in_specs=(
            P("ex", None, "hid"),
            P("ex", None, "hid"),
            P("ex", None),
            P("hid", None),
            P("hid", None),
            P(),
            P(),
            P("ex", "hid"),
        ),
        out_specs=P("ex", "hid"),
        check_vma=False,
    )
```

```python
import functools

import jax
import jax.numpy as jnp
from jax import lax
from jax.experimental import pallas as pl
from jax.experimental.pallas import tpu as pltpu
from jax.sharding import PartitionSpec as P

F32 = jnp.float32
BF16 = jnp.bfloat16
NT = (((1,), (1,)), ((), ()))
TN = (((0,), (0,)), ((), ()))
VMEM = pl.BlockSpec(memory_space=pltpu.VMEM)
HBM = pl.BlockSpec(memory_space=pltpu.HBM)
HIGH = lax.Precision.HIGHEST


def params(mib):
    return pltpu.CompilerParams(vmem_limit_bytes=mib << 20)


def hbm(x):
    return pltpu.with_memory_space_constraint(x, pltpu.HBM)


def out_kernel(chunks, x_hbm, w_hbm, out_ref, sent_ref, x_ref, wide_ref, tall_ref, sems):
    rows = x_hbm.shape[0]
    step = rows // chunks
    weights = pltpu.make_async_copy(w_hbm, wide_ref, sems.at[chunks])
    weights.start()
    copies = [
        pltpu.make_async_copy(
            x_hbm.at[pl.ds(c * step, step)], x_ref.at[pl.ds(c * step, step)], sems.at[c]
        )
        for c in range(chunks)
    ]
    for copy in copies:
        copy.start()
    weights.wait()
    tall_ref[...] = wide_ref[...].T
    half = rows // 2
    rank = w_hbm.shape[0]
    for side in range(2):
        for copy in copies[side * chunks // 2 : (side + 1) * chunks // 2]:
            copy.wait()
        part = jnp.dot(
            x_ref[pl.ds(side * half, half), :], tall_ref[...], preferred_element_type=F32
        )
        out_ref[:, pl.ds(side * rank, rank)] = part
        sent_ref[:, pl.ds(side * rank, rank)] = part.astype(BF16)


def project_out(x, w_t, chunks):
    rows, depth = x.shape
    rank = w_t.shape[0]
    shape = (rows // 2, 2 * rank)
    return pl.pallas_call(
        functools.partial(out_kernel, chunks),
        out_shape=[jax.ShapeDtypeStruct(shape, F32), jax.ShapeDtypeStruct(shape, BF16)],
        in_specs=[HBM, HBM],
        out_specs=[VMEM] * 2,
        scratch_shapes=[
            pltpu.VMEM((rows, depth), BF16),
            pltpu.VMEM((rank, depth), BF16),
            pltpu.VMEM((depth, rank), BF16),
            pltpu.SemaphoreType.DMA((chunks + 1,)),
        ],
        compiler_params=params(16),
        cost_estimate=pl.CostEstimate(
            flops=60 * rows * depth * rank, bytes_accessed=60 * rows * depth, transcendentals=0
        ),
    )(hbm(x), hbm(w_t))


def in_kernel(x_ref, w_ref, out_ref, tall_ref):
    half = x_ref.shape[0] // 2
    rank = w_ref.shape[0]
    tall_ref[...] = w_ref[...].T
    for side in range(2):
        part = jnp.dot(
            x_ref[pl.ds(side * half, half), :], tall_ref[...], preferred_element_type=F32
        )
        out_ref[:, pl.ds(side * rank, rank)] = part


def project_in(x, w_t):
    rows, depth = x.shape
    rank = w_t.shape[0]
    return pl.pallas_call(
        in_kernel,
        out_shape=jax.ShapeDtypeStruct((rows // 2, 2 * rank), F32),
        in_specs=[VMEM, VMEM],
        out_specs=VMEM,
        scratch_shapes=[pltpu.VMEM((depth, rank), BF16)],
        compiler_params=params(16),
        cost_estimate=pl.CostEstimate(
            flops=2 * rows * depth * rank, bytes_accessed=2 * rows * depth, transcendentals=0
        ),
    )(x, w_t)


def outer_kernel(
    length, in_ref, own_ref, got_ref, mask_ref, inv_ref, part_ref, sent_ref, rows_ref, pairs_ref
):
    rank = inv_ref.shape[0]
    seqs = mask_ref.shape[0]
    counts = jnp.sum(mask_ref[...].astype(F32), axis=1, keepdims=True)
    lane = lax.broadcasted_iota(jnp.int32, (length, 2 * rank), 1)
    token = lax.broadcasted_iota(jnp.int32, (length, 2 * rank), 0).astype(F32)
    grams = [None] * seqs
    for pair in range(seqs // 2):
        rows = pl.ds(pair * length, length)
        low, high = counts[pair : pair + 1, :], counts[pair + seqs // 2 : pair + seqs // 2 + 1, :]
        real = token < jnp.where(lane < rank, low, high)
        inside = jnp.where(real, in_ref[rows, :], 0.0)
        outside = own_ref[rows, :] + got_ref[rows, :].astype(F32)
        both = lax.dot_general(
            inside, outside, TN, precision=HIGH, preferred_element_type=F32
        )
        grams[pair] = both[:rank, :rank] / low
        grams[pair + seqs // 2] = both[rank:, rank:] / high
    gram = jnp.concatenate(grams, axis=1)
    pre = lax.dot_general(inv_ref[...], gram, TN, precision=HIGH, preferred_element_type=F32)
    half = rank // 2
    for s in range(seqs):
        rows_ref[...] = pre[:, s * rank : (s + 1) * rank]
        pairs_ref[pl.ds(s * half, half), :] = jnp.concatenate(
            [rows_ref[pl.ds(0, half, stride=2), :], rows_ref[pl.ds(1, half, stride=2), :]], axis=1
        )
    for b in range(half):
        row = pairs_ref[pl.ds(b, seqs, stride=half), :]
        part_ref[:, pl.ds(b * 2 * rank, 2 * rank)] = row
    sent_ref[...] = part_ref[...].astype(BF16)


def outer(in_part, out_own, out_got, token_mask, inv_input):
    seqs, length = token_mask.shape
    rank = inv_input.shape[0]
    shape = (seqs, rank * rank)
    return pl.pallas_call(
        functools.partial(outer_kernel, length),
        out_shape=[jax.ShapeDtypeStruct(shape, F32), jax.ShapeDtypeStruct(shape, BF16)],
        in_specs=[VMEM] * 5,
        out_specs=[VMEM] * 2,
        scratch_shapes=[
            pltpu.VMEM((rank, rank), F32),
            pltpu.VMEM((seqs * rank // 2, 2 * rank), F32),
        ],
        compiler_params=params(16),
    )(in_part, out_own, out_got, token_mask, inv_input)


def query_kernel(query_ref, inv_ref, pre_ref):
    rank = inv_ref.shape[0]
    zero = jnp.zeros((rank, rank), F32)
    inv = inv_ref[...]
    block = jnp.concatenate(
        [jnp.concatenate([inv, zero], axis=1), jnp.concatenate([zero, inv], axis=1)], axis=0
    )
    top = block.astype(BF16)
    rest = block - top.astype(F32)
    middle = rest.astype(BF16)
    last = (rest - middle.astype(F32)).astype(BF16)
    for b in range(query_ref.shape[1] // (2 * rank)):
        lanes = pl.ds(b * 2 * rank, 2 * rank)
        query = query_ref[:, lanes]
        total = jnp.dot(query, last, preferred_element_type=F32)
        total += jnp.dot(query, middle, preferred_element_type=F32)
        total += jnp.dot(query, top, preferred_element_type=F32)
        pre_ref[:, lanes] = total.astype(BF16)


def precondition_queries(query_feats, inv_output):
    return pl.pallas_call(
        query_kernel,
        out_shape=jax.ShapeDtypeStruct(query_feats.shape, BF16),
        in_specs=[VMEM] * 2,
        out_specs=VMEM,
        compiler_params=params(16),
    )(query_feats, inv_output)


def score_kernel(place_ref, low_ref, high_ref, *rest):
    *pieces, out_ref, feats_ref = rest
    seqs = pieces[0].shape[0]
    for k, piece in enumerate(pieces):
        feats_ref[pl.ds(k * seqs, seqs), :] = piece[...].astype(F32)
    half = low_ref.shape[1]
    feats = feats_ref[...].astype(BF16)
    scores = lax.dot_general(low_ref[...], feats[:, :half], NT, preferred_element_type=F32)
    scores += lax.dot_general(high_ref[...], feats[:, half:], NT, preferred_element_type=F32)
    scores = scores.T
    rows = scores.shape[0]
    at = lax.broadcasted_iota(jnp.int32, scores.shape, 0)
    size = seqs
    while size < rows:
        swapped = jnp.where(
            (at & size) == 0, pltpu.roll(scores, rows - size, 0), pltpu.roll(scores, size, 0)
        )
        bit = (place_ref[...] & (size // seqs)) != 0
        scores = jnp.where(bit, swapped, scores)
        size *= 2
    out_ref[...] = scores


def score(place, low, high, pieces):
    seqs, feats = pieces[0].shape
    rows = seqs * len(pieces)
    return pl.pallas_call(
        score_kernel,
        out_shape=jax.ShapeDtypeStruct((rows, low.shape[0]), F32),
        in_specs=[VMEM] * (3 + len(pieces)),
        out_specs=VMEM,
        scratch_shapes=[pltpu.VMEM((rows, feats), F32)],
        compiler_params=params(16),
    )(place, low, high, *pieces)


def local_pair(
    activations, out_grads, token_mask, proj_in, proj_out, inv_input, inv_output, query_feats
):
    seqs, length, depth = activations.shape
    ex_size = lax.axis_size("ex")
    ex = lax.axis_index("ex")
    hid = lax.axis_index("hid")
    half = ex_size // 2
    swap_hid = [(0, 1), (1, 0)]

    out_own, out_sent = project_out(out_grads.reshape(seqs * length, -1), proj_out.T, 4)
    out_got = lax.ppermute(out_sent, "hid", swap_hid)
    in_part = project_in(activations.reshape(seqs * length, depth), proj_in.T)
    part, sent = outer(in_part, out_own, out_got, token_mask, inv_input)

    around, across = [], []
    for e in range(half):
        a, b, c, d = 2 * e + 1, 2 * e, 2 * (e + half), 2 * (e + half) + 1
        around += [(a, b), (b, c), (c, d), (d, a)]
        across += [(a, c), (c, a), (b, b ^ 2), (d, d ^ 2)]
    axes = ("ex", "hid")
    second = lax.ppermute(sent, axes, across)
    first = lax.ppermute(sent, axes, around)
    home = (ex // half) == hid
    mine = (
        first.astype(F32) + jnp.where(home, part, second.astype(F32))
    ).astype(BF16)

    query_own = precondition_queries(query_feats, inv_output)
    query_got = lax.ppermute(query_own, "hid", swap_hid)
    low = jnp.where(hid == 0, query_own, query_got)
    high = jnp.where(hid == 0, query_got, query_own)

    pieces = [mine]
    far = [k for k in range(2, half, 2)]
    pieces = {0: mine}
    for k in sorted(far, key=lambda k: -k):
        pieces[k] = lax.ppermute(mine, "ex", [(i, i ^ k) for i in range(ex_size)])
    for k in list(pieces):
        pieces[k ^ 1] = lax.ppermute(pieces[k], "ex", [(i, i ^ 1) for i in range(ex_size)])
    place = jnp.full((seqs * half, query_feats.shape[0]), ex % half, jnp.int32)
    scores = score(place, low, high, [pieces[k] for k in range(half)])
    return scores.T


def local_any(
    activations, out_grads, token_mask, proj_in, proj_out, inv_input, inv_output, query_feats
):
    seq_count, length, unit_local = activations.shape
    rank_width = proj_in.shape[1]
    hid_size = lax.axis_size("hid")
    row_block = rank_width // hid_size
    my_index = lax.axis_index("hid")
    in_part = jnp.dot(
        activations.reshape(seq_count * length, unit_local),
        proj_in,
        preferred_element_type=F32,
    )
    in_part = jnp.dot(in_part, inv_input, precision=HIGH)
    out_part = jnp.dot(
        out_grads.reshape(seq_count * length, out_grads.shape[2]),
        proj_out,
        preferred_element_type=F32,
    )
    token_weight = token_mask.astype(F32)
    tok_count = jnp.sum(token_weight, axis=1)
    in_full, out_full = lax.psum((in_part, out_part), "hid")
    in_mine = lax.dynamic_slice_in_dim(in_full, my_index * row_block, row_block, 1)
    masked = in_mine.reshape(seq_count, length, row_block) * token_weight[:, :, None]
    outer_sum = jnp.einsum(
        "slr,slq->srq",
        masked,
        out_full.reshape(seq_count, length, rank_width),
        precision=HIGH,
    )
    train_feats = (
        (outer_sum / tok_count[:, None, None])
        .astype(BF16)
        .reshape(seq_count, row_block * rank_width)
    )
    query_count = query_feats.shape[0]
    queries = query_feats.reshape(query_count, row_block, rank_width).astype(F32)
    query_pre = jnp.einsum("qij,jk->qik", queries, inv_output, precision=HIGH)
    query_pre = query_pre.astype(BF16).reshape(query_count, row_block * rank_width)
    partial_value = jnp.einsum(
        "qk,tk->qt",
        query_pre,
        lax.all_gather(train_feats, "ex", axis=0, tiled=True),
        preferred_element_type=F32,
    )
    return lax.psum_scatter(partial_value, "hid", scatter_dimension=1, tiled=True)


def solution(mesh):
    ex_size, hid_size = mesh.shape["ex"], mesh.shape["hid"]
    paired = hid_size == 2 and ex_size >= 4 and ex_size & (ex_size - 1) == 0
    return jax.shard_map(
        local_pair if paired else local_any,
        mesh=mesh,
        in_specs=(
            P("ex", None, "hid"),
            P("ex", None, "hid"),
            P("ex", None),
            P("hid", None),
            P("hid", None),
            P(),
            P(),
            P("ex", "hid"),
        ),
        out_specs=P("ex", "hid"),
        check_vma=False,
    )
```

```python
import functools

import jax
import jax.numpy as jnp
from jax import lax
from jax.experimental import pallas as pl
from jax.experimental.pallas import tpu as pltpu
from jax.sharding import PartitionSpec as P

F32 = jnp.float32
BF16 = jnp.bfloat16
NT = (((1,), (1,)), ((), ()))
TN = (((0,), (0,)), ((), ()))
VMEM = pl.BlockSpec(memory_space=pltpu.VMEM)
HBM = pl.BlockSpec(memory_space=pltpu.HBM)
HIGH = lax.Precision.HIGHEST


def params(mib):
    return pltpu.CompilerParams(vmem_limit_bytes=mib << 20)


def hbm(x):
    return pltpu.with_memory_space_constraint(x, pltpu.HBM)


def precondition(query_ref, inv_ref, block_ref, pre_ref):
    rank = inv_ref.shape[0]
    block_ref[...] = jnp.zeros_like(block_ref)
    block_ref[pl.ds(0, rank), pl.ds(0, rank)] = inv_ref[...]
    block_ref[pl.ds(rank, rank), pl.ds(rank, rank)] = inv_ref[...]
    block = block_ref[...]
    top = block.astype(BF16)
    rest = block - top.astype(F32)
    middle = rest.astype(BF16)
    last = (rest - middle.astype(F32)).astype(BF16)
    for b in range(query_ref.shape[1] // (2 * rank)):
        lanes = pl.ds(b * 2 * rank, 2 * rank)
        query = query_ref[:, lanes]
        total = jnp.dot(query, last, preferred_element_type=F32)
        total += jnp.dot(query, middle, preferred_element_type=F32)
        total += jnp.dot(query, top, preferred_element_type=F32)
        pre_ref[:, lanes] = total.astype(BF16)


def out_kernel(
    chunks, x_hbm, w_hbm, query_hbm, inv_hbm, out_ref, sent_ref, pre_ref,
    x_ref, wide_ref, tall_ref, query_ref, inv_ref, block_ref, sems,
):
    rows = x_hbm.shape[0]
    step = rows // chunks
    weights = pltpu.make_async_copy(w_hbm, wide_ref, sems.at[chunks])
    inverse = pltpu.make_async_copy(inv_hbm, inv_ref, sems.at[chunks + 1])
    queries = pltpu.make_async_copy(query_hbm, query_ref, sems.at[chunks + 2])
    inverse.start()
    queries.start()
    weights.start()
    copies = [
        pltpu.make_async_copy(
            x_hbm.at[pl.ds(c * step, step)], x_ref.at[pl.ds(c * step, step)], sems.at[c]
        )
        for c in range(chunks)
    ]
    for copy in copies:
        copy.start()
    inverse.wait()
    queries.wait()
    precondition(query_ref, inv_ref, block_ref, pre_ref)
    weights.wait()
    tall_ref[...] = wide_ref[...].T
    half = rows // 2
    rank = w_hbm.shape[0]
    for side in range(2):
        for copy in copies[side * chunks // 2 : (side + 1) * chunks // 2]:
            copy.wait()
        part = jnp.dot(
            x_ref[pl.ds(side * half, half), :], tall_ref[...], preferred_element_type=F32
        )
        out_ref[:, pl.ds(side * rank, rank)] = part
        sent_ref[:, pl.ds(side * rank, rank)] = part.astype(BF16)


def project_out(x, w_t, query, inv, chunks):
    rows, depth = x.shape
    rank = w_t.shape[0]
    shape = (rows // 2, 2 * rank)
    return pl.pallas_call(
        functools.partial(out_kernel, chunks),
        out_shape=[
            jax.ShapeDtypeStruct(shape, F32),
            jax.ShapeDtypeStruct(shape, BF16),
            jax.ShapeDtypeStruct(query.shape, BF16),
        ],
        in_specs=[HBM] * 4,
        out_specs=[VMEM] * 3,
        scratch_shapes=[
            pltpu.VMEM((rows, depth), BF16),
            pltpu.VMEM((rank, depth), BF16),
            pltpu.VMEM((depth, rank), BF16),
            pltpu.VMEM(query.shape, BF16),
            pltpu.VMEM(inv.shape, F32),
            pltpu.VMEM((2 * rank, 2 * rank), F32),
            pltpu.SemaphoreType.DMA((chunks + 3,)),
        ],
        compiler_params=params(16),
        cost_estimate=pl.CostEstimate(
            flops=60 * rows * depth * rank, bytes_accessed=60 * rows * depth, transcendentals=0
        ),
    )(hbm(x), hbm(w_t), hbm(query), hbm(inv))


def in_kernel(x_ref, w_ref, out_ref, tall_ref):
    half = x_ref.shape[0] // 2
    rank = w_ref.shape[0]
    tall_ref[...] = w_ref[...].T
    for side in range(2):
        part = jnp.dot(
            x_ref[pl.ds(side * half, half), :], tall_ref[...], preferred_element_type=F32
        )
        out_ref[:, pl.ds(side * rank, rank)] = part


def project_in(x, w_t):
    rows, depth = x.shape
    rank = w_t.shape[0]
    return pl.pallas_call(
        in_kernel,
        out_shape=jax.ShapeDtypeStruct((rows // 2, 2 * rank), F32),
        in_specs=[VMEM, VMEM],
        out_specs=VMEM,
        scratch_shapes=[pltpu.VMEM((depth, rank), BF16)],
        compiler_params=params(16),
        cost_estimate=pl.CostEstimate(
            flops=2 * rows * depth * rank, bytes_accessed=2 * rows * depth, transcendentals=0
        ),
    )(x, w_t)


def outer_kernel(
    length, in_ref, own_ref, got_ref, mask_ref, inv_ref, part_ref, sent_ref, rows_ref, pairs_ref
):
    rank = inv_ref.shape[0]
    seqs = mask_ref.shape[0]
    counts = jnp.sum(mask_ref[...].astype(F32), axis=1, keepdims=True)
    lane = lax.broadcasted_iota(jnp.int32, (length, 2 * rank), 1)
    token = lax.broadcasted_iota(jnp.int32, (length, 2 * rank), 0).astype(F32)
    grams = [None] * seqs
    for pair in range(seqs // 2):
        rows = pl.ds(pair * length, length)
        low, high = counts[pair : pair + 1, :], counts[pair + seqs // 2 : pair + seqs // 2 + 1, :]
        real = token < jnp.where(lane < rank, low, high)
        inside = jnp.where(real, in_ref[rows, :], 0.0)
        outside = own_ref[rows, :] + got_ref[rows, :].astype(F32)
        both = lax.dot_general(
            inside, outside, TN, precision=HIGH, preferred_element_type=F32
        )
        grams[pair] = both[:rank, :rank] / low
        grams[pair + seqs // 2] = both[rank:, rank:] / high
    gram = jnp.concatenate(grams, axis=1)
    pre = lax.dot_general(inv_ref[...], gram, TN, precision=HIGH, preferred_element_type=F32)
    half = rank // 2
    for s in range(seqs):
        rows_ref[...] = pre[:, s * rank : (s + 1) * rank]
        pairs_ref[pl.ds(s * half, half), :] = jnp.concatenate(
            [rows_ref[pl.ds(0, half, stride=2), :], rows_ref[pl.ds(1, half, stride=2), :]], axis=1
        )
    for b in range(half):
        row = pairs_ref[pl.ds(b, seqs, stride=half), :]
        part_ref[:, pl.ds(b * 2 * rank, 2 * rank)] = row
    sent_ref[...] = part_ref[...].astype(BF16)


def outer(in_part, out_own, out_got, token_mask, inv_input):
    seqs, length = token_mask.shape
    rank = inv_input.shape[0]
    shape = (seqs, rank * rank)
    return pl.pallas_call(
        functools.partial(outer_kernel, length),
        out_shape=[jax.ShapeDtypeStruct(shape, F32), jax.ShapeDtypeStruct(shape, BF16)],
        in_specs=[VMEM] * 5,
        out_specs=[VMEM] * 2,
        scratch_shapes=[
            pltpu.VMEM((rank, rank), F32),
            pltpu.VMEM((seqs * rank // 2, 2 * rank), F32),
        ],
        compiler_params=params(16),
    )(in_part, out_own, out_got, token_mask, inv_input)


def pass_kernel(x_ref, y_ref):
    y_ref[...] = x_ref[...]


def pass_on(x):
    return pl.pallas_call(
        pass_kernel,
        out_shape=jax.ShapeDtypeStruct(x.shape, x.dtype),
        in_specs=[VMEM],
        out_specs=VMEM,
        compiler_params=params(16),
    )(x)


def score_kernel(place_ref, low_ref, high_ref, *rest):
    *pieces, out_ref, feats_ref = rest
    seqs = pieces[0].shape[0]
    for k, piece in enumerate(pieces):
        feats_ref[pl.ds(k * seqs, seqs), :] = piece[...].astype(F32)
    half = low_ref.shape[1]
    feats = feats_ref[...].astype(BF16)
    scores = lax.dot_general(low_ref[...], feats[:, :half], NT, preferred_element_type=F32)
    scores += lax.dot_general(high_ref[...], feats[:, half:], NT, preferred_element_type=F32)
    scores = scores.T
    rows = scores.shape[0]
    at = lax.broadcasted_iota(jnp.int32, scores.shape, 0)
    size = seqs
    while size < rows:
        swapped = jnp.where(
            (at & size) == 0, pltpu.roll(scores, rows - size, 0), pltpu.roll(scores, size, 0)
        )
        bit = (place_ref[...] & (size // seqs)) != 0
        scores = jnp.where(bit, swapped, scores)
        size *= 2
    out_ref[...] = scores


def score(place, low, high, pieces):
    seqs, feats = pieces[0].shape
    rows = seqs * len(pieces)
    return pl.pallas_call(
        score_kernel,
        out_shape=jax.ShapeDtypeStruct((rows, low.shape[0]), F32),
        in_specs=[VMEM] * (3 + len(pieces)),
        out_specs=VMEM,
        scratch_shapes=[pltpu.VMEM((rows, feats), F32)],
        compiler_params=params(16),
    )(place, low, high, *pieces)


def local_pair(
    activations, out_grads, token_mask, proj_in, proj_out, inv_input, inv_output, query_feats
):
    seqs, length, depth = activations.shape
    ex_size = lax.axis_size("ex")
    ex = lax.axis_index("ex")
    hid = lax.axis_index("hid")
    half = ex_size // 2
    swap_hid = [(0, 1), (1, 0)]

    out_own, out_sent, query_own = project_out(
        out_grads.reshape(seqs * length, -1), proj_out.T, query_feats, inv_output, 4
    )
    out_got = lax.ppermute(out_sent, "hid", swap_hid)
    in_part = project_in(activations.reshape(seqs * length, depth), proj_in.T)
    part, sent = outer(in_part, out_own, out_got, token_mask, inv_input)

    alpha, beta = [], []
    for e in range(half):
        a, b, c, d = 2 * e + 1, 2 * e, 2 * (e + half), 2 * (e + half) + 1
        alpha += [(a, b), (b, c), (c, a), (d, d ^ 2)]
        beta += [(c, d), (d, a), (a, c), (b, b ^ 2)]
    axes = ("ex", "hid")
    second = lax.ppermute(sent, axes, beta)
    first = lax.ppermute(sent, axes, alpha)
    home = (ex // half) == hid
    mine = (
        jnp.where(home & (hid == 0), part, second.astype(F32))
        + jnp.where(home & (hid == 1), part, first.astype(F32))
    ).astype(BF16)

    query_own = pass_on(query_own)
    query_got = lax.ppermute(query_own, "hid", swap_hid)
    low = jnp.where(hid == 0, query_own, query_got)
    high = jnp.where(hid == 0, query_got, query_own)

    pieces = [mine]
    far = [k for k in range(2, half, 2)]
    pieces = {0: mine}
    for k in sorted(far, key=lambda k: -k):
        pieces[k] = lax.ppermute(mine, "ex", [(i, i ^ k) for i in range(ex_size)])
    for k in list(pieces):
        pieces[k ^ 1] = lax.ppermute(pieces[k], "ex", [(i, i ^ 1) for i in range(ex_size)])
    place = jnp.full((seqs * half, query_feats.shape[0]), ex % half, jnp.int32)
    scores = score(place, low, high, [pieces[k] for k in range(half)])
    return scores.T


def local_any(
    activations, out_grads, token_mask, proj_in, proj_out, inv_input, inv_output, query_feats
):
    seq_count, length, unit_local = activations.shape
    rank_width = proj_in.shape[1]
    hid_size = lax.axis_size("hid")
    row_block = rank_width // hid_size
    my_index = lax.axis_index("hid")
    in_part = jnp.dot(
        activations.reshape(seq_count * length, unit_local),
        proj_in,
        preferred_element_type=F32,
    )
    in_part = jnp.dot(in_part, inv_input, precision=HIGH)
    out_part = jnp.dot(
        out_grads.reshape(seq_count * length, out_grads.shape[2]),
        proj_out,
        preferred_element_type=F32,
    )
    token_weight = token_mask.astype(F32)
    tok_count = jnp.sum(token_weight, axis=1)
    in_full, out_full = lax.psum((in_part, out_part), "hid")
    in_mine = lax.dynamic_slice_in_dim(in_full, my_index * row_block, row_block, 1)
    masked = in_mine.reshape(seq_count, length, row_block) * token_weight[:, :, None]
    outer_sum = jnp.einsum(
        "slr,slq->srq",
        masked,
        out_full.reshape(seq_count, length, rank_width),
        precision=HIGH,
    )
    train_feats = (
        (outer_sum / tok_count[:, None, None])
        .astype(BF16)
        .reshape(seq_count, row_block * rank_width)
    )
    query_count = query_feats.shape[0]
    queries = query_feats.reshape(query_count, row_block, rank_width).astype(F32)
    query_pre = jnp.einsum("qij,jk->qik", queries, inv_output, precision=HIGH)
    query_pre = query_pre.astype(BF16).reshape(query_count, row_block * rank_width)
    partial_value = jnp.einsum(
        "qk,tk->qt",
        query_pre,
        lax.all_gather(train_feats, "ex", axis=0, tiled=True),
        preferred_element_type=F32,
    )
    return lax.psum_scatter(partial_value, "hid", scatter_dimension=1, tiled=True)


def solution(mesh):
    ex_size, hid_size = mesh.shape["ex"], mesh.shape["hid"]
    paired = hid_size == 2 and ex_size >= 4 and ex_size & (ex_size - 1) == 0
    return jax.shard_map(
        local_pair if paired else local_any,
        mesh=mesh,
        in_specs=(
            P("ex", None, "hid"),
            P("ex", None, "hid"),
            P("ex", None),
            P("hid", None),
            P("hid", None),
            P(),
            P(),
            P("ex", "hid"),
        ),
        out_specs=P("ex", "hid"),
        check_vma=False,
    )
```

```python
import functools

import jax
import jax.numpy as jnp
from jax import lax
from jax.experimental import pallas as pl
from jax.experimental.pallas import tpu as pltpu
from jax.sharding import PartitionSpec as P

F32 = jnp.float32
BF16 = jnp.bfloat16
NT = (((1,), (1,)), ((), ()))
TN = (((0,), (0,)), ((), ()))
VMEM = pl.BlockSpec(memory_space=pltpu.VMEM)
HBM = pl.BlockSpec(memory_space=pltpu.HBM)
HIGH = lax.Precision.HIGHEST


def params(mib):
    return pltpu.CompilerParams(vmem_limit_bytes=mib << 20)


def hbm(x):
    return pltpu.with_memory_space_constraint(x, pltpu.HBM)


def precondition(query_ref, inv_ref, block_ref, pre_ref):
    rank = inv_ref.shape[0]
    block_ref[...] = jnp.zeros_like(block_ref)
    block_ref[pl.ds(0, rank), pl.ds(0, rank)] = inv_ref[...]
    block_ref[pl.ds(rank, rank), pl.ds(rank, rank)] = inv_ref[...]
    block = block_ref[...]
    top = block.astype(BF16)
    rest = block - top.astype(F32)
    middle = rest.astype(BF16)
    last = (rest - middle.astype(F32)).astype(BF16)
    for b in range(query_ref.shape[1] // (2 * rank)):
        lanes = pl.ds(b * 2 * rank, 2 * rank)
        query = query_ref[:, lanes]
        total = jnp.dot(query, last, preferred_element_type=F32)
        total += jnp.dot(query, middle, preferred_element_type=F32)
        total += jnp.dot(query, top, preferred_element_type=F32)
        pre_ref[:, lanes] = total.astype(BF16)


def out_kernel(
    chunks, x_hbm, w_hbm, query_hbm, inv_hbm, out_ref, sent_ref, pre_ref,
    x_ref, wide_ref, tall_ref, query_ref, inv_ref, block_ref, sems,
):
    rows = x_hbm.shape[0]
    step = rows // chunks
    weights = pltpu.make_async_copy(w_hbm, wide_ref, sems.at[chunks])
    inverse = pltpu.make_async_copy(inv_hbm, inv_ref, sems.at[chunks + 1])
    queries = pltpu.make_async_copy(query_hbm, query_ref, sems.at[chunks + 2])
    inverse.start()
    queries.start()
    weights.start()
    copies = [
        pltpu.make_async_copy(
            x_hbm.at[pl.ds(c * step, step)], x_ref.at[pl.ds(c * step, step)], sems.at[c]
        )
        for c in range(chunks)
    ]
    for copy in copies:
        copy.start()
    inverse.wait()
    queries.wait()
    precondition(query_ref, inv_ref, block_ref, pre_ref)
    weights.wait()
    tall_ref[...] = wide_ref[...].T
    half = rows // 2
    rank = w_hbm.shape[0]
    for side in range(2):
        for copy in copies[side * chunks // 2 : (side + 1) * chunks // 2]:
            copy.wait()
        part = jnp.dot(
            x_ref[pl.ds(side * half, half), :], tall_ref[...], preferred_element_type=F32
        )
        out_ref[:, pl.ds(side * rank, rank)] = part
        sent_ref[:, pl.ds(side * rank, rank)] = part.astype(BF16)


def project_out(x, w_t, query, inv, chunks):
    rows, depth = x.shape
    rank = w_t.shape[0]
    shape = (rows // 2, 2 * rank)
    return pl.pallas_call(
        functools.partial(out_kernel, chunks),
        out_shape=[
            jax.ShapeDtypeStruct(shape, F32),
            jax.ShapeDtypeStruct(shape, BF16),
            jax.ShapeDtypeStruct(query.shape, BF16),
        ],
        in_specs=[HBM] * 4,
        out_specs=[VMEM] * 3,
        scratch_shapes=[
            pltpu.VMEM((rows, depth), BF16),
            pltpu.VMEM((rank, depth), BF16),
            pltpu.VMEM((depth, rank), BF16),
            pltpu.VMEM(query.shape, BF16),
            pltpu.VMEM(inv.shape, F32),
            pltpu.VMEM((2 * rank, 2 * rank), F32),
            pltpu.SemaphoreType.DMA((chunks + 3,)),
        ],
        compiler_params=params(16),
        cost_estimate=pl.CostEstimate(
            flops=60 * rows * depth * rank, bytes_accessed=60 * rows * depth, transcendentals=0
        ),
    )(hbm(x), hbm(w_t), hbm(query), hbm(inv))


def in_kernel(x_ref, w_ref, out_ref, tall_ref):
    half = x_ref.shape[0] // 2
    rank = w_ref.shape[0]
    tall_ref[...] = w_ref[...].T
    for side in range(2):
        part = jnp.dot(
            x_ref[pl.ds(side * half, half), :], tall_ref[...], preferred_element_type=F32
        )
        out_ref[:, pl.ds(side * rank, rank)] = part


def project_in(x, w_t):
    rows, depth = x.shape
    rank = w_t.shape[0]
    return pl.pallas_call(
        in_kernel,
        out_shape=jax.ShapeDtypeStruct((rows // 2, 2 * rank), F32),
        in_specs=[VMEM, VMEM],
        out_specs=VMEM,
        scratch_shapes=[pltpu.VMEM((depth, rank), BF16)],
        compiler_params=params(16),
        cost_estimate=pl.CostEstimate(
            flops=2 * rows * depth * rank, bytes_accessed=2 * rows * depth, transcendentals=0
        ),
    )(x, w_t)


def split(x):
    top = x.astype(BF16)
    return top, (x - top.astype(F32)).astype(BF16)


def precise_dot(a, b, dims):
    (top_a, rest_a), (top_b, rest_b) = split(a), split(b)
    axis_a, axis_b = dims
    return lax.dot_general(
        jnp.concatenate([top_a, top_a, rest_a], axis=axis_a),
        jnp.concatenate([top_b, rest_b, top_b], axis=axis_b),
        (((axis_a,), (axis_b,)), ((), ())),
        preferred_element_type=F32,
    )


def outer_kernel(
    length, in_ref, own_ref, got_ref, mask_ref, inv_ref, part_ref, sent_ref, pairs_ref
):
    rank = inv_ref.shape[0]
    seqs = mask_ref.shape[0]
    half = rank // 2
    counts = jnp.sum(mask_ref[...].astype(F32), axis=1, keepdims=True)
    lane = lax.broadcasted_iota(jnp.int32, (length, 2 * rank), 1)
    token = lax.broadcasted_iota(jnp.int32, (length, 2 * rank), 0).astype(F32)
    grams = [None] * seqs
    for pair in range(seqs // 2):
        rows = pl.ds(pair * length, length)
        low, high = counts[pair : pair + 1, :], counts[pair + seqs // 2 : pair + seqs // 2 + 1, :]
        real = token < jnp.where(lane < rank, low, high)
        inside = jnp.where(real, in_ref[rows, :], 0.0)
        outside = own_ref[rows, :] + got_ref[rows, :].astype(F32)
        both = precise_dot(inside, outside, (0, 0))
        grams[pair] = both[:rank, :rank] / low
        grams[pair + seqs // 2] = both[rank:, rank:] / high
    gram = jnp.concatenate(grams, axis=1)
    mixed = jnp.concatenate(
        [inv_ref[pl.ds(0, half, stride=2), :], inv_ref[pl.ds(1, half, stride=2), :]], axis=0
    )
    pre = precise_dot(mixed, gram, (1, 0))
    for s in range(seqs):
        one = pre[:, s * rank : (s + 1) * rank]
        pairs_ref[pl.ds(s * half, half), :] = jnp.concatenate([one[:half], one[half:]], axis=1)
    for b in range(half):
        row = pairs_ref[pl.ds(b, seqs, stride=half), :]
        lanes = pl.ds(b * 2 * rank, 2 * rank)
        part_ref[:, lanes] = row
        sent_ref[:, lanes] = row.astype(BF16)


def outer(in_part, out_own, out_got, token_mask, inv_input):
    seqs, length = token_mask.shape
    rank = inv_input.shape[0]
    shape = (seqs, rank * rank)
    return pl.pallas_call(
        functools.partial(outer_kernel, length),
        out_shape=[jax.ShapeDtypeStruct(shape, F32), jax.ShapeDtypeStruct(shape, BF16)],
        in_specs=[VMEM] * 5,
        out_specs=[VMEM] * 2,
        scratch_shapes=[
            pltpu.VMEM((seqs * rank // 2, 2 * rank), F32),
        ],
        compiler_params=params(16),
    )(in_part, out_own, out_got, token_mask, inv_input)


def pass_kernel(x_ref, y_ref):
    y_ref[...] = x_ref[...]


def pass_on(x):
    return pl.pallas_call(
        pass_kernel,
        out_shape=jax.ShapeDtypeStruct(x.shape, x.dtype),
        in_specs=[VMEM],
        out_specs=VMEM,
        compiler_params=params(16),
    )(x)


def score_kernel(place_ref, low_ref, high_ref, *rest):
    *pieces, out_ref, feats_ref = rest
    seqs = pieces[0].shape[0]
    for k, piece in enumerate(pieces):
        feats_ref[pl.ds(k * seqs, seqs), :] = piece[...].astype(F32)
    half = low_ref.shape[1]
    feats = feats_ref[...].astype(BF16)
    scores = lax.dot_general(low_ref[...], feats[:, :half], NT, preferred_element_type=F32)
    scores += lax.dot_general(high_ref[...], feats[:, half:], NT, preferred_element_type=F32)
    scores = scores.T
    rows = scores.shape[0]
    at = lax.broadcasted_iota(jnp.int32, scores.shape, 0)
    size = seqs
    while size < rows:
        swapped = jnp.where(
            (at & size) == 0, pltpu.roll(scores, rows - size, 0), pltpu.roll(scores, size, 0)
        )
        bit = (place_ref[...] & (size // seqs)) != 0
        scores = jnp.where(bit, swapped, scores)
        size *= 2
    out_ref[...] = scores


def score(place, low, high, pieces):
    seqs, feats = pieces[0].shape
    rows = seqs * len(pieces)
    return pl.pallas_call(
        score_kernel,
        out_shape=jax.ShapeDtypeStruct((rows, low.shape[0]), F32),
        in_specs=[VMEM] * (3 + len(pieces)),
        out_specs=VMEM,
        scratch_shapes=[pltpu.VMEM((rows, feats), F32)],
        compiler_params=params(16),
    )(place, low, high, *pieces)


def local_pair(
    activations, out_grads, token_mask, proj_in, proj_out, inv_input, inv_output, query_feats
):
    seqs, length, depth = activations.shape
    ex_size = lax.axis_size("ex")
    ex = lax.axis_index("ex")
    hid = lax.axis_index("hid")
    half = ex_size // 2
    swap_hid = [(0, 1), (1, 0)]

    out_own, out_sent, query_own = project_out(
        out_grads.reshape(seqs * length, -1), proj_out.T, query_feats, inv_output, 4
    )
    out_got = lax.ppermute(out_sent, "hid", swap_hid)
    in_part = project_in(activations.reshape(seqs * length, depth), proj_in.T)
    part, sent = outer(in_part, out_own, out_got, token_mask, inv_input)

    alpha, beta = [], []
    for e in range(half):
        a, b, c, d = 2 * e + 1, 2 * e, 2 * (e + half), 2 * (e + half) + 1
        alpha += [(a, b), (b, c), (c, a), (d, d ^ 2)]
        beta += [(c, d), (d, a), (a, c), (b, b ^ 2)]
    axes = ("ex", "hid")
    second = lax.ppermute(sent, axes, beta)
    first = lax.ppermute(sent, axes, alpha)
    home = (ex // half) == hid
    mine = (
        jnp.where(home & (hid == 0), part, second.astype(F32))
        + jnp.where(home & (hid == 1), part, first.astype(F32))
    ).astype(BF16)

    query_own = pass_on(query_own)
    query_got = lax.ppermute(query_own, "hid", swap_hid)
    low = jnp.where(hid == 0, query_own, query_got)
    high = jnp.where(hid == 0, query_got, query_own)

    pieces = [mine]
    far = [k for k in range(2, half, 2)]
    pieces = {0: mine}
    for k in sorted(far, key=lambda k: -k):
        pieces[k] = lax.ppermute(mine, "ex", [(i, i ^ k) for i in range(ex_size)])
    for k in list(pieces):
        pieces[k ^ 1] = lax.ppermute(pieces[k], "ex", [(i, i ^ 1) for i in range(ex_size)])
    place = jnp.full((seqs * half, query_feats.shape[0]), ex % half, jnp.int32)
    scores = score(place, low, high, [pieces[k] for k in range(half)])
    return scores.T


def local_any(
    activations, out_grads, token_mask, proj_in, proj_out, inv_input, inv_output, query_feats
):
    seq_count, length, unit_local = activations.shape
    rank_width = proj_in.shape[1]
    hid_size = lax.axis_size("hid")
    row_block = rank_width // hid_size
    my_index = lax.axis_index("hid")
    in_part = jnp.dot(
        activations.reshape(seq_count * length, unit_local),
        proj_in,
        preferred_element_type=F32,
    )
    in_part = jnp.dot(in_part, inv_input, precision=HIGH)
    out_part = jnp.dot(
        out_grads.reshape(seq_count * length, out_grads.shape[2]),
        proj_out,
        preferred_element_type=F32,
    )
    token_weight = token_mask.astype(F32)
    tok_count = jnp.sum(token_weight, axis=1)
    in_full, out_full = lax.psum((in_part, out_part), "hid")
    in_mine = lax.dynamic_slice_in_dim(in_full, my_index * row_block, row_block, 1)
    masked = in_mine.reshape(seq_count, length, row_block) * token_weight[:, :, None]
    outer_sum = jnp.einsum(
        "slr,slq->srq",
        masked,
        out_full.reshape(seq_count, length, rank_width),
        precision=HIGH,
    )
    train_feats = (
        (outer_sum / tok_count[:, None, None])
        .astype(BF16)
        .reshape(seq_count, row_block * rank_width)
    )
    query_count = query_feats.shape[0]
    queries = query_feats.reshape(query_count, row_block, rank_width).astype(F32)
    query_pre = jnp.einsum("qij,jk->qik", queries, inv_output, precision=HIGH)
    query_pre = query_pre.astype(BF16).reshape(query_count, row_block * rank_width)
    partial_value = jnp.einsum(
        "qk,tk->qt",
        query_pre,
        lax.all_gather(train_feats, "ex", axis=0, tiled=True),
        preferred_element_type=F32,
    )
    return lax.psum_scatter(partial_value, "hid", scatter_dimension=1, tiled=True)


def solution(mesh):
    ex_size, hid_size = mesh.shape["ex"], mesh.shape["hid"]
    paired = hid_size == 2 and ex_size >= 4 and ex_size & (ex_size - 1) == 0
    return jax.shard_map(
        local_pair if paired else local_any,
        mesh=mesh,
        in_specs=(
            P("ex", None, "hid"),
            P("ex", None, "hid"),
            P("ex", None),
            P("hid", None),
            P("hid", None),
            P(),
            P(),
            P("ex", "hid"),
        ),
        out_specs=P("ex", "hid"),
        check_vma=False,
    )
```

```python
import functools

import jax
import jax.numpy as jnp
from jax import lax
from jax.experimental import pallas as pl
from jax.experimental.pallas import tpu as pltpu
from jax.sharding import PartitionSpec as P

F32 = jnp.float32
BF16 = jnp.bfloat16
NT = (((1,), (1,)), ((), ()))
TN = (((0,), (0,)), ((), ()))
VMEM = pl.BlockSpec(memory_space=pltpu.VMEM)
HBM = pl.BlockSpec(memory_space=pltpu.HBM)
HIGH = lax.Precision.HIGHEST


def params(mib):
    return pltpu.CompilerParams(vmem_limit_bytes=mib << 20)


def hbm(x):
    return pltpu.with_memory_space_constraint(x, pltpu.HBM)


def precondition(query_ref, inv_ref, block_ref, pre_ref):
    rank = inv_ref.shape[0]
    block_ref[...] = jnp.zeros_like(block_ref)
    block_ref[pl.ds(0, rank), pl.ds(0, rank)] = inv_ref[...]
    block_ref[pl.ds(rank, rank), pl.ds(rank, rank)] = inv_ref[...]
    block = block_ref[...]
    top = block.astype(BF16)
    rest = block - top.astype(F32)
    middle = rest.astype(BF16)
    last = (rest - middle.astype(F32)).astype(BF16)
    for b in range(query_ref.shape[1] // (2 * rank)):
        lanes = pl.ds(b * 2 * rank, 2 * rank)
        query = query_ref[:, lanes]
        total = jnp.dot(query, last, preferred_element_type=F32)
        total += jnp.dot(query, middle, preferred_element_type=F32)
        total += jnp.dot(query, top, preferred_element_type=F32)
        pre_ref[:, lanes] = total.astype(BF16)


def out_kernel(
    chunks, x_hbm, w_hbm, query_hbm, inv_hbm, out_ref, sent_ref, pre_ref,
    x_ref, wide_ref, tall_ref, query_ref, inv_ref, block_ref, sems,
):
    rows = x_hbm.shape[0]
    step = rows // chunks
    weights = pltpu.make_async_copy(w_hbm, wide_ref, sems.at[chunks])
    inverse = pltpu.make_async_copy(inv_hbm, inv_ref, sems.at[chunks + 1])
    queries = pltpu.make_async_copy(query_hbm, query_ref, sems.at[chunks + 2])
    inverse.start()
    queries.start()
    weights.start()
    copies = [
        pltpu.make_async_copy(
            x_hbm.at[pl.ds(c * step, step)], x_ref.at[pl.ds(c * step, step)], sems.at[c]
        )
        for c in range(chunks)
    ]
    for copy in copies:
        copy.start()
    inverse.wait()
    queries.wait()
    precondition(query_ref, inv_ref, block_ref, pre_ref)
    weights.wait()
    tall_ref[...] = wide_ref[...].T
    half = rows // 2
    rank = w_hbm.shape[0]
    for side in range(2):
        for copy in copies[side * chunks // 2 : (side + 1) * chunks // 2]:
            copy.wait()
        part = jnp.dot(
            x_ref[pl.ds(side * half, half), :], tall_ref[...], preferred_element_type=F32
        )
        out_ref[:, pl.ds(side * rank, rank)] = part
        sent_ref[:, pl.ds(side * rank, rank)] = part.astype(BF16)


def project_out(x, w_t, query, inv, chunks):
    rows, depth = x.shape
    rank = w_t.shape[0]
    shape = (rows // 2, 2 * rank)
    return pl.pallas_call(
        functools.partial(out_kernel, chunks),
        out_shape=[
            jax.ShapeDtypeStruct(shape, F32),
            jax.ShapeDtypeStruct(shape, BF16),
            jax.ShapeDtypeStruct(query.shape, BF16),
        ],
        in_specs=[HBM] * 4,
        out_specs=[VMEM] * 3,
        scratch_shapes=[
            pltpu.VMEM((rows, depth), BF16),
            pltpu.VMEM((rank, depth), BF16),
            pltpu.VMEM((depth, rank), BF16),
            pltpu.VMEM(query.shape, BF16),
            pltpu.VMEM(inv.shape, F32),
            pltpu.VMEM((2 * rank, 2 * rank), F32),
            pltpu.SemaphoreType.DMA((chunks + 3,)),
        ],
        compiler_params=params(16),
        cost_estimate=pl.CostEstimate(
            flops=60 * rows * depth * rank, bytes_accessed=60 * rows * depth, transcendentals=0
        ),
    )(hbm(x), hbm(w_t), hbm(query), hbm(inv))


def in_kernel(x_ref, w_ref, out_ref, tall_ref):
    half = x_ref.shape[0] // 2
    rank = w_ref.shape[0]
    tall_ref[...] = w_ref[...].T
    for side in range(2):
        part = jnp.dot(
            x_ref[pl.ds(side * half, half), :], tall_ref[...], preferred_element_type=F32
        )
        out_ref[:, pl.ds(side * rank, rank)] = part


def project_in(x, w_t):
    rows, depth = x.shape
    rank = w_t.shape[0]
    return pl.pallas_call(
        in_kernel,
        out_shape=jax.ShapeDtypeStruct((rows // 2, 2 * rank), F32),
        in_specs=[VMEM, VMEM],
        out_specs=VMEM,
        scratch_shapes=[pltpu.VMEM((depth, rank), BF16)],
        compiler_params=params(16),
        cost_estimate=pl.CostEstimate(
            flops=2 * rows * depth * rank, bytes_accessed=2 * rows * depth, transcendentals=0
        ),
    )(x, w_t)


def split(x):
    top = x.astype(BF16)
    return top, (x - top.astype(F32)).astype(BF16)


def precise_dot(a, b, dims):
    (top_a, rest_a), (top_b, rest_b) = split(a), split(b)
    axis_a, axis_b = dims
    return lax.dot_general(
        jnp.concatenate([top_a, top_a, rest_a], axis=axis_a),
        jnp.concatenate([top_b, rest_b, top_b], axis=axis_b),
        (((axis_a,), (axis_b,)), ((), ())),
        preferred_element_type=F32,
    )


def outer_kernel(
    length, in_ref, own_ref, got_ref, mask_ref, inv_ref, part_ref, sent_ref, pairs_ref
):
    rank = inv_ref.shape[0]
    seqs = mask_ref.shape[0]
    half = rank // 2
    counts = jnp.sum(mask_ref[...].astype(F32), axis=1, keepdims=True)
    lane = lax.broadcasted_iota(jnp.int32, (length, 2 * rank), 1)
    token = lax.broadcasted_iota(jnp.int32, (length, 2 * rank), 0).astype(F32)
    grams = [None] * seqs
    for pair in range(seqs // 2):
        rows = pl.ds(pair * length, length)
        low, high = counts[pair : pair + 1, :], counts[pair + seqs // 2 : pair + seqs // 2 + 1, :]
        real = token < jnp.where(lane < rank, low, high)
        inside = jnp.where(real, in_ref[rows, :], 0.0)
        outside = own_ref[rows, :] + got_ref[rows, :].astype(F32)
        both = precise_dot(inside, outside, (0, 0))
        grams[pair] = both[:rank, :rank] / low
        grams[pair + seqs // 2] = both[rank:, rank:] / high
    gram = jnp.concatenate(grams, axis=1)
    mixed = jnp.concatenate(
        [inv_ref[pl.ds(0, half, stride=2), :], inv_ref[pl.ds(1, half, stride=2), :]], axis=0
    )
    pre = precise_dot(mixed, gram, (1, 0))
    for s in range(seqs):
        one = pre[:, s * rank : (s + 1) * rank]
        pairs_ref[pl.ds(s * half, half), :] = jnp.concatenate([one[:half], one[half:]], axis=1)
    for b in range(half):
        row = pairs_ref[pl.ds(b, seqs, stride=half), :]
        lanes = pl.ds(b * 2 * rank, 2 * rank)
        part_ref[:, lanes] = row
        sent_ref[:, lanes] = row.astype(BF16)


def outer(in_part, out_own, out_got, token_mask, inv_input):
    seqs, length = token_mask.shape
    rank = inv_input.shape[0]
    shape = (seqs, rank * rank)
    return pl.pallas_call(
        functools.partial(outer_kernel, length),
        out_shape=[jax.ShapeDtypeStruct(shape, F32), jax.ShapeDtypeStruct(shape, BF16)],
        in_specs=[VMEM] * 5,
        out_specs=[VMEM] * 2,
        scratch_shapes=[
            pltpu.VMEM((seqs * rank // 2, 2 * rank), F32),
        ],
        compiler_params=params(16),
    )(in_part, out_own, out_got, token_mask, inv_input)


def pass_kernel(x_ref, y_ref):
    y_ref[...] = x_ref[...]


def pass_on(x):
    return pl.pallas_call(
        pass_kernel,
        out_shape=jax.ShapeDtypeStruct(x.shape, x.dtype),
        in_specs=[VMEM],
        out_specs=VMEM,
        compiler_params=params(16),
    )(x)


def score_kernel(place_ref, low_ref, high_ref, *rest):
    *pieces, out_ref, feats_ref = rest
    seqs = pieces[0].shape[0]
    for k, piece in enumerate(pieces):
        feats_ref[pl.ds(k * seqs, seqs), :] = piece[...].astype(F32)
    half = low_ref.shape[1]
    feats = feats_ref[...].astype(BF16)
    scores = lax.dot_general(low_ref[...], feats[:, :half], NT, preferred_element_type=F32)
    scores += lax.dot_general(high_ref[...], feats[:, half:], NT, preferred_element_type=F32)
    scores = scores.T
    rows = scores.shape[0]
    at = lax.broadcasted_iota(jnp.int32, scores.shape, 0)
    size = seqs
    while size < rows:
        swapped = jnp.where(
            (at & size) == 0, pltpu.roll(scores, rows - size, 0), pltpu.roll(scores, size, 0)
        )
        bit = (place_ref[...] & (size // seqs)) != 0
        scores = jnp.where(bit, swapped, scores)
        size *= 2
    out_ref[...] = scores


def score(place, low, high, pieces):
    seqs, feats = pieces[0].shape
    rows = seqs * len(pieces)
    return pl.pallas_call(
        score_kernel,
        out_shape=jax.ShapeDtypeStruct((rows, low.shape[0]), F32),
        in_specs=[VMEM] * (3 + len(pieces)),
        out_specs=VMEM,
        scratch_shapes=[pltpu.VMEM((rows, feats), F32)],
        compiler_params=params(16),
    )(place, low, high, *pieces)


def local_pair(
    activations, out_grads, token_mask, proj_in, proj_out, inv_input, inv_output, query_feats
):
    seqs, length, depth = activations.shape
    ex_size = lax.axis_size("ex")
    ex = lax.axis_index("ex")
    hid = lax.axis_index("hid")
    half = ex_size // 2
    swap_hid = [(0, 1), (1, 0)]

    out_own, out_sent, query_own = project_out(
        out_grads.reshape(seqs * length, -1), proj_out.T, query_feats, inv_output, 4
    )
    out_got = lax.ppermute(out_sent, "hid", swap_hid)
    in_part = project_in(activations.reshape(seqs * length, depth), proj_in.T)
    part, sent = outer(in_part, out_own, out_got, token_mask, inv_input)

    alpha, beta = [], []
    for e in range(half):
        a, b, c, d = 2 * e + 1, 2 * e, 2 * (e + half), 2 * (e + half) + 1
        alpha += [(a, b), (b, c ^ 2), (c, a ^ 2), (d, d ^ 2)]
        beta += [(c, d), (d, a ^ 2), (a, c ^ 2), (b, b ^ 2)]
    axes = ("ex", "hid")
    second = lax.ppermute(sent, axes, beta)
    first = lax.ppermute(sent, axes, alpha)
    home = (ex // half) == hid
    mine = (
        jnp.where(home & (hid == 0), part, second.astype(F32))
        + jnp.where(home & (hid == 1), part, first.astype(F32))
    ).astype(BF16)

    query_own = pass_on(query_own)
    query_got = lax.ppermute(query_own, "hid", swap_hid)
    low = jnp.where(hid == 0, query_own, query_got)
    high = jnp.where(hid == 0, query_got, query_own)

    pieces = {0: mine}
    for k in range(half - 1, 1, -2):
        pieces[k] = lax.ppermute(mine, "ex", [(i, i ^ k) for i in range(ex_size)])
    for k in list(pieces):
        pieces[k ^ 1] = lax.ppermute(pieces[k], "ex", [(i, i ^ 1) for i in range(ex_size)])
    place = jnp.full((seqs * half, query_feats.shape[0]), ex % half ^ jnp.where(home, 0, 1), jnp.int32)
    scores = score(place, low, high, [pieces[k] for k in range(half)])
    return scores.T


def local_any(
    activations, out_grads, token_mask, proj_in, proj_out, inv_input, inv_output, query_feats
):
    seq_count, length, unit_local = activations.shape
    rank_width = proj_in.shape[1]
    hid_size = lax.axis_size("hid")
    row_block = rank_width // hid_size
    my_index = lax.axis_index("hid")
    in_part = jnp.dot(
        activations.reshape(seq_count * length, unit_local),
        proj_in,
        preferred_element_type=F32,
    )
    in_part = jnp.dot(in_part, inv_input, precision=HIGH)
    out_part = jnp.dot(
        out_grads.reshape(seq_count * length, out_grads.shape[2]),
        proj_out,
        preferred_element_type=F32,
    )
    token_weight = token_mask.astype(F32)
    tok_count = jnp.sum(token_weight, axis=1)
    in_full, out_full = lax.psum((in_part, out_part), "hid")
    in_mine = lax.dynamic_slice_in_dim(in_full, my_index * row_block, row_block, 1)
    masked = in_mine.reshape(seq_count, length, row_block) * token_weight[:, :, None]
    outer_sum = jnp.einsum(
        "slr,slq->srq",
        masked,
        out_full.reshape(seq_count, length, rank_width),
        precision=HIGH,
    )
    train_feats = (
        (outer_sum / tok_count[:, None, None])
        .astype(BF16)
        .reshape(seq_count, row_block * rank_width)
    )
    query_count = query_feats.shape[0]
    queries = query_feats.reshape(query_count, row_block, rank_width).astype(F32)
    query_pre = jnp.einsum("qij,jk->qik", queries, inv_output, precision=HIGH)
    query_pre = query_pre.astype(BF16).reshape(query_count, row_block * rank_width)
    partial_value = jnp.einsum(
        "qk,tk->qt",
        query_pre,
        lax.all_gather(train_feats, "ex", axis=0, tiled=True),
        preferred_element_type=F32,
    )
    return lax.psum_scatter(partial_value, "hid", scatter_dimension=1, tiled=True)


def solution(mesh):
    ex_size, hid_size = mesh.shape["ex"], mesh.shape["hid"]
    paired = hid_size == 2 and ex_size >= 4 and ex_size & (ex_size - 1) == 0
    return jax.shard_map(
        local_pair if paired else local_any,
        mesh=mesh,
        in_specs=(
            P("ex", None, "hid"),
            P("ex", None, "hid"),
            P("ex", None),
            P("hid", None),
            P("hid", None),
            P(),
            P(),
            P("ex", "hid"),
        ),
        out_specs=P("ex", "hid"),
        check_vma=False,
    )
```

```python
import functools

import jax
import jax.numpy as jnp
from jax import lax
from jax.experimental import pallas as pl
from jax.experimental.pallas import tpu as pltpu
from jax.sharding import PartitionSpec as P

F32 = jnp.float32
BF16 = jnp.bfloat16
NT = (((1,), (1,)), ((), ()))
TN = (((0,), (0,)), ((), ()))
VMEM = pl.BlockSpec(memory_space=pltpu.VMEM)
HBM = pl.BlockSpec(memory_space=pltpu.HBM)
HIGH = lax.Precision.HIGHEST


def params(mib):
    return pltpu.CompilerParams(vmem_limit_bytes=mib << 20)


def hbm(x):
    return pltpu.with_memory_space_constraint(x, pltpu.HBM)


def precondition(query_ref, inv_ref, block_ref, pre_ref):
    rank = inv_ref.shape[0]
    block_ref[...] = jnp.zeros_like(block_ref)
    block_ref[pl.ds(0, rank), pl.ds(0, rank)] = inv_ref[...]
    block_ref[pl.ds(rank, rank), pl.ds(rank, rank)] = inv_ref[...]
    block = block_ref[...]
    top = block.astype(BF16)
    rest = block - top.astype(F32)
    middle = rest.astype(BF16)
    last = (rest - middle.astype(F32)).astype(BF16)
    for b in range(query_ref.shape[1] // (2 * rank)):
        lanes = pl.ds(b * 2 * rank, 2 * rank)
        query = query_ref[:, lanes]
        total = jnp.dot(query, last, preferred_element_type=F32)
        total += jnp.dot(query, middle, preferred_element_type=F32)
        total += jnp.dot(query, top, preferred_element_type=F32)
        pre_ref[:, lanes] = total.astype(BF16)


def out_kernel(
    chunks, x_hbm, w_hbm, query_hbm, inv_hbm, out_ref, sent_ref, pre_ref,
    x_ref, wide_ref, tall_ref, query_ref, inv_ref, block_ref, sems,
):
    rows = x_hbm.shape[0]
    step = rows // chunks
    weights = pltpu.make_async_copy(w_hbm, wide_ref, sems.at[chunks])
    inverse = pltpu.make_async_copy(inv_hbm, inv_ref, sems.at[chunks + 1])
    queries = pltpu.make_async_copy(query_hbm, query_ref, sems.at[chunks + 2])
    inverse.start()
    queries.start()
    weights.start()
    copies = [
        pltpu.make_async_copy(
            x_hbm.at[pl.ds(c * step, step)], x_ref.at[pl.ds(c * step, step)], sems.at[c]
        )
        for c in range(chunks)
    ]
    for copy in copies:
        copy.start()
    inverse.wait()
    queries.wait()
    precondition(query_ref, inv_ref, block_ref, pre_ref)
    weights.wait()
    tall_ref[...] = wide_ref[...].T
    half = rows // 2
    rank = w_hbm.shape[0]
    for side in range(2):
        for copy in copies[side * chunks // 2 : (side + 1) * chunks // 2]:
            copy.wait()
        part = jnp.dot(
            x_ref[pl.ds(side * half, half), :], tall_ref[...], preferred_element_type=F32
        )
        out_ref[:, pl.ds(side * rank, rank)] = part
        sent_ref[:, pl.ds(side * rank, rank)] = part.astype(BF16)


def project_out(x, w_t, query, inv, chunks):
    rows, depth = x.shape
    rank = w_t.shape[0]
    shape = (rows // 2, 2 * rank)
    return pl.pallas_call(
        functools.partial(out_kernel, chunks),
        out_shape=[
            jax.ShapeDtypeStruct(shape, F32),
            jax.ShapeDtypeStruct(shape, BF16),
            jax.ShapeDtypeStruct(query.shape, BF16),
        ],
        in_specs=[HBM] * 4,
        out_specs=[VMEM] * 3,
        scratch_shapes=[
            pltpu.VMEM((rows, depth), BF16),
            pltpu.VMEM((rank, depth), BF16),
            pltpu.VMEM((depth, rank), BF16),
            pltpu.VMEM(query.shape, BF16),
            pltpu.VMEM(inv.shape, F32),
            pltpu.VMEM((2 * rank, 2 * rank), F32),
            pltpu.SemaphoreType.DMA((chunks + 3,)),
        ],
        compiler_params=params(16),
        cost_estimate=pl.CostEstimate(
            flops=60 * rows * depth * rank, bytes_accessed=60 * rows * depth, transcendentals=0
        ),
    )(hbm(x), hbm(w_t), hbm(query), hbm(inv))


def in_kernel(x_ref, w_ref, out_ref, tall_ref):
    half = x_ref.shape[0] // 2
    rank = w_ref.shape[0]
    tall_ref[...] = w_ref[...].T
    for side in range(2):
        part = jnp.dot(
            x_ref[pl.ds(side * half, half), :], tall_ref[...], preferred_element_type=F32
        )
        out_ref[:, pl.ds(side * rank, rank)] = part


def project_in(x, w_t):
    rows, depth = x.shape
    rank = w_t.shape[0]
    return pl.pallas_call(
        in_kernel,
        out_shape=jax.ShapeDtypeStruct((rows // 2, 2 * rank), F32),
        in_specs=[VMEM, VMEM],
        out_specs=VMEM,
        scratch_shapes=[pltpu.VMEM((depth, rank), BF16)],
        compiler_params=params(16),
        cost_estimate=pl.CostEstimate(
            flops=2 * rows * depth * rank, bytes_accessed=2 * rows * depth, transcendentals=0
        ),
    )(x, w_t)


def split(x):
    top = x.astype(BF16)
    return top, (x - top.astype(F32)).astype(BF16)


def precise_dot(a, b, dims):
    (top_a, rest_a), (top_b, rest_b) = split(a), split(b)
    axis_a, axis_b = dims
    return lax.dot_general(
        jnp.concatenate([top_a, top_a, rest_a], axis=axis_a),
        jnp.concatenate([top_b, rest_b, top_b], axis=axis_b),
        (((axis_a,), (axis_b,)), ((), ())),
        preferred_element_type=F32,
    )


def outer_kernel(
    length, in_ref, own_ref, got_ref, mask_ref, inv_ref, part_ref, sent_ref, pairs_ref
):
    rank = inv_ref.shape[0]
    seqs = mask_ref.shape[0]
    half = rank // 2
    counts = jnp.sum(mask_ref[...].astype(F32), axis=1, keepdims=True)
    lane = lax.broadcasted_iota(jnp.int32, (length, 2 * rank), 1)
    token = lax.broadcasted_iota(jnp.int32, (length, 2 * rank), 0).astype(F32)
    grams = [None] * seqs
    for pair in range(seqs // 2):
        rows = pl.ds(pair * length, length)
        low, high = counts[pair : pair + 1, :], counts[pair + seqs // 2 : pair + seqs // 2 + 1, :]
        real = token < jnp.where(lane < rank, low, high)
        inside = jnp.where(real, in_ref[rows, :], 0.0)
        outside = own_ref[rows, :] + got_ref[rows, :].astype(F32)
        both = precise_dot(inside, outside, (0, 0))
        grams[pair] = both[:rank, :rank] / low
        grams[pair + seqs // 2] = both[rank:, rank:] / high
    gram = jnp.concatenate(grams, axis=1)
    mixed = jnp.concatenate(
        [inv_ref[pl.ds(0, half, stride=2), :], inv_ref[pl.ds(1, half, stride=2), :]], axis=0
    )
    pre = precise_dot(mixed, gram, (1, 0))
    for s in range(seqs):
        one = pre[:, s * rank : (s + 1) * rank]
        pairs_ref[pl.ds(s * half, half), :] = jnp.concatenate([one[:half], one[half:]], axis=1)
    for b in range(half):
        row = pairs_ref[pl.ds(b, seqs, stride=half), :]
        lanes = pl.ds(b * 2 * rank, 2 * rank)
        part_ref[:, lanes] = row
        sent_ref[:, lanes] = row.astype(BF16)


def outer(in_part, out_own, out_got, token_mask, inv_input):
    seqs, length = token_mask.shape
    rank = inv_input.shape[0]
    shape = (seqs, rank * rank)
    return pl.pallas_call(
        functools.partial(outer_kernel, length),
        out_shape=[jax.ShapeDtypeStruct(shape, F32), jax.ShapeDtypeStruct(shape, BF16)],
        in_specs=[VMEM] * 5,
        out_specs=[VMEM] * 2,
        scratch_shapes=[
            pltpu.VMEM((seqs * rank // 2, 2 * rank), F32),
        ],
        compiler_params=params(16),
    )(in_part, out_own, out_got, token_mask, inv_input)


def pass_kernel(x_ref, y_ref):
    y_ref[...] = x_ref[...]


def pass_on(x):
    return pl.pallas_call(
        pass_kernel,
        out_shape=jax.ShapeDtypeStruct(x.shape, x.dtype),
        in_specs=[VMEM],
        out_specs=VMEM,
        compiler_params=params(16),
    )(x)


def score_kernel(place_ref, low_ref, high_ref, *rest):
    *pieces, out_ref, feats_ref = rest
    seqs = pieces[0].shape[0]
    for k, piece in enumerate(pieces):
        feats_ref[pl.ds(k * seqs, seqs), :] = piece[...].astype(F32)
    half = low_ref.shape[1]
    feats = feats_ref[...].astype(BF16)
    scores = lax.dot_general(low_ref[...], feats[:, :half], NT, preferred_element_type=F32)
    scores += lax.dot_general(high_ref[...], feats[:, half:], NT, preferred_element_type=F32)
    scores = scores.T
    rows = scores.shape[0]
    at = lax.broadcasted_iota(jnp.int32, scores.shape, 0)
    size = seqs
    while size < rows:
        swapped = jnp.where(
            (at & size) == 0, pltpu.roll(scores, rows - size, 0), pltpu.roll(scores, size, 0)
        )
        bit = (place_ref[...] & (size // seqs)) != 0
        scores = jnp.where(bit, swapped, scores)
        size *= 2
    out_ref[...] = scores


def score(place, low, high, pieces):
    seqs, feats = pieces[0].shape
    rows = seqs * len(pieces)
    return pl.pallas_call(
        score_kernel,
        out_shape=jax.ShapeDtypeStruct((rows, low.shape[0]), F32),
        in_specs=[VMEM] * (3 + len(pieces)),
        out_specs=VMEM,
        scratch_shapes=[pltpu.VMEM((rows, feats), F32)],
        compiler_params=params(16),
    )(place, low, high, *pieces)


def local_pair(
    activations, out_grads, token_mask, proj_in, proj_out, inv_input, inv_output, query_feats
):
    seqs, length, depth = activations.shape
    ex_size = lax.axis_size("ex")
    ex = lax.axis_index("ex")
    hid = lax.axis_index("hid")
    half = ex_size // 2
    swap_hid = [(0, 1), (1, 0)]

    out_own, out_sent, query_own = project_out(
        out_grads.reshape(seqs * length, -1), proj_out.T, query_feats, inv_output, 4
    )
    out_got = lax.ppermute(out_sent, "hid", swap_hid)
    in_part = project_in(activations.reshape(seqs * length, depth), proj_in.T)
    part, sent = outer(in_part, out_own, out_got, token_mask, inv_input)

    alpha, beta = [], []
    for e in range(half):
        a, b, c, d = 2 * e + 1, 2 * e, 2 * (e + half), 2 * (e + half) + 1
        alpha += [(a, b), (b, c ^ 2), (c, a ^ 2), (d, d ^ 2)]
        beta += [(c, d), (d, a ^ 2), (a, c ^ 2), (b, b ^ 2)]
    axes = ("ex", "hid")
    second = lax.ppermute(sent, axes, beta)
    first = lax.ppermute(sent, axes, alpha)
    home = (ex // half) == hid
    mine = (
        jnp.where(home & (hid == 0), part, second.astype(F32))
        + jnp.where(home & (hid == 1), part, first.astype(F32))
    ).astype(BF16)

    query_own = pass_on(query_own)
    query_got = lax.ppermute(query_own, "hid", swap_hid)
    low = jnp.where(hid == 0, query_own, query_got)
    high = jnp.where(hid == 0, query_got, query_own)

    pieces = {0: mine}
    for k in range(half - 2, 0, -2):
        k = k if k & (k - 1) else k ^ 1
        pieces[k] = lax.ppermute(mine, "ex", [(i, i ^ k) for i in range(ex_size)])
    for k in list(pieces):
        pieces[k ^ 1] = lax.ppermute(pieces[k], "ex", [(i, i ^ 1) for i in range(ex_size)])
    place = jnp.full((seqs * half, query_feats.shape[0]), ex % half ^ jnp.where(home, 0, 1), jnp.int32)
    scores = score(place, low, high, [pieces[k] for k in range(half)])
    return scores.T


def local_any(
    activations, out_grads, token_mask, proj_in, proj_out, inv_input, inv_output, query_feats
):
    seq_count, length, unit_local = activations.shape
    rank_width = proj_in.shape[1]
    hid_size = lax.axis_size("hid")
    row_block = rank_width // hid_size
    my_index = lax.axis_index("hid")
    in_part = jnp.dot(
        activations.reshape(seq_count * length, unit_local),
        proj_in,
        preferred_element_type=F32,
    )
    in_part = jnp.dot(in_part, inv_input, precision=HIGH)
    out_part = jnp.dot(
        out_grads.reshape(seq_count * length, out_grads.shape[2]),
        proj_out,
        preferred_element_type=F32,
    )
    token_weight = token_mask.astype(F32)
    tok_count = jnp.sum(token_weight, axis=1)
    in_full, out_full = lax.psum((in_part, out_part), "hid")
    in_mine = lax.dynamic_slice_in_dim(in_full, my_index * row_block, row_block, 1)
    masked = in_mine.reshape(seq_count, length, row_block) * token_weight[:, :, None]
    outer_sum = jnp.einsum(
        "slr,slq->srq",
        masked,
        out_full.reshape(seq_count, length, rank_width),
        precision=HIGH,
    )
    train_feats = (
        (outer_sum / tok_count[:, None, None])
        .astype(BF16)
        .reshape(seq_count, row_block * rank_width)
    )
    query_count = query_feats.shape[0]
    queries = query_feats.reshape(query_count, row_block, rank_width).astype(F32)
    query_pre = jnp.einsum("qij,jk->qik", queries, inv_output, precision=HIGH)
    query_pre = query_pre.astype(BF16).reshape(query_count, row_block * rank_width)
    partial_value = jnp.einsum(
        "qk,tk->qt",
        query_pre,
        lax.all_gather(train_feats, "ex", axis=0, tiled=True),
        preferred_element_type=F32,
    )
    return lax.psum_scatter(partial_value, "hid", scatter_dimension=1, tiled=True)


def solution(mesh):
    ex_size, hid_size = mesh.shape["ex"], mesh.shape["hid"]
    paired = hid_size == 2 and ex_size >= 4 and ex_size & (ex_size - 1) == 0
    return jax.shard_map(
        local_pair if paired else local_any,
        mesh=mesh,
        in_specs=(
            P("ex", None, "hid"),
            P("ex", None, "hid"),
            P("ex", None),
            P("hid", None),
            P("hid", None),
            P(),
            P(),
            P("ex", "hid"),
        ),
        out_specs=P("ex", "hid"),
        check_vma=False,
    )
```

```python
import functools

import jax
import jax.numpy as jnp
from jax import lax
from jax.experimental import pallas as pl
from jax.experimental.pallas import tpu as pltpu
from jax.sharding import PartitionSpec as P

F32 = jnp.float32
BF16 = jnp.bfloat16
NT = (((1,), (1,)), ((), ()))
TN = (((0,), (0,)), ((), ()))
VMEM = pl.BlockSpec(memory_space=pltpu.VMEM)
HBM = pl.BlockSpec(memory_space=pltpu.HBM)
HIGH = lax.Precision.HIGHEST


def params(mib):
    return pltpu.CompilerParams(vmem_limit_bytes=mib << 20)


def hbm(x):
    return pltpu.with_memory_space_constraint(x, pltpu.HBM)


def precondition(query_ref, inv_ref, block_ref, pre_ref):
    rank = inv_ref.shape[0]
    block_ref[...] = jnp.zeros_like(block_ref)
    block_ref[pl.ds(0, rank), pl.ds(0, rank)] = inv_ref[...]
    block_ref[pl.ds(rank, rank), pl.ds(rank, rank)] = inv_ref[...]
    block = block_ref[...]
    top = block.astype(BF16)
    rest = block - top.astype(F32)
    middle = rest.astype(BF16)
    last = (rest - middle.astype(F32)).astype(BF16)
    count, feats = query_ref.shape
    width = 2 * rank
    tiles = feats // width
    stacked = jnp.concatenate(
        [query_ref[:, b * width : (b + 1) * width] for b in range(tiles)], axis=0
    )
    terms = jnp.dot(
        stacked, jnp.concatenate([last, middle, top], axis=1), preferred_element_type=F32
    )
    total = terms[:, :width] + terms[:, width : 2 * width] + terms[:, 2 * width :]
    for b in range(tiles):
        tile = total[b * count : (b + 1) * count]
        pre_ref[:, pl.ds(b * width, width)] = tile.astype(BF16)


def out_kernel(
    chunks, x_hbm, w_hbm, query_hbm, inv_hbm, out_ref, sent_ref, pre_ref,
    x_ref, wide_ref, tall_ref, query_ref, inv_ref, block_ref, sems,
):
    rows = x_hbm.shape[0]
    step = rows // chunks
    weights = pltpu.make_async_copy(w_hbm, wide_ref, sems.at[chunks])
    inverse = pltpu.make_async_copy(inv_hbm, inv_ref, sems.at[chunks + 1])
    queries = pltpu.make_async_copy(query_hbm, query_ref, sems.at[chunks + 2])
    inverse.start()
    queries.start()
    weights.start()
    copies = [
        pltpu.make_async_copy(
            x_hbm.at[pl.ds(c * step, step)], x_ref.at[pl.ds(c * step, step)], sems.at[c]
        )
        for c in range(chunks)
    ]
    for copy in copies:
        copy.start()
    inverse.wait()
    queries.wait()
    precondition(query_ref, inv_ref, block_ref, pre_ref)
    weights.wait()
    tall_ref[...] = wide_ref[...].T
    half = rows // 2
    rank = w_hbm.shape[0]
    for side in range(2):
        for copy in copies[side * chunks // 2 : (side + 1) * chunks // 2]:
            copy.wait()
        part = jnp.dot(
            x_ref[pl.ds(side * half, half), :], tall_ref[...], preferred_element_type=F32
        )
        out_ref[:, pl.ds(side * rank, rank)] = part
        sent_ref[:, pl.ds(side * rank, rank)] = part.astype(BF16)


def project_out(x, w_t, query, inv, chunks):
    rows, depth = x.shape
    rank = w_t.shape[0]
    shape = (rows // 2, 2 * rank)
    return pl.pallas_call(
        functools.partial(out_kernel, chunks),
        out_shape=[
            jax.ShapeDtypeStruct(shape, F32),
            jax.ShapeDtypeStruct(shape, BF16),
            jax.ShapeDtypeStruct(query.shape, BF16),
        ],
        in_specs=[HBM] * 4,
        out_specs=[VMEM] * 3,
        scratch_shapes=[
            pltpu.VMEM((rows, depth), BF16),
            pltpu.VMEM((rank, depth), BF16),
            pltpu.VMEM((depth, rank), BF16),
            pltpu.VMEM(query.shape, BF16),
            pltpu.VMEM(inv.shape, F32),
            pltpu.VMEM((2 * rank, 2 * rank), F32),
            pltpu.SemaphoreType.DMA((chunks + 3,)),
        ],
        compiler_params=params(16),
        cost_estimate=pl.CostEstimate(
            flops=60 * rows * depth * rank, bytes_accessed=60 * rows * depth, transcendentals=0
        ),
    )(hbm(x), hbm(w_t), hbm(query), hbm(inv))


def in_kernel(x_ref, w_ref, out_ref, tall_ref):
    half = x_ref.shape[0] // 2
    rank = w_ref.shape[0]
    tall_ref[...] = w_ref[...].T
    for side in range(2):
        part = jnp.dot(
            x_ref[pl.ds(side * half, half), :], tall_ref[...], preferred_element_type=F32
        )
        out_ref[:, pl.ds(side * rank, rank)] = part


def project_in(x, w_t):
    rows, depth = x.shape
    rank = w_t.shape[0]
    return pl.pallas_call(
        in_kernel,
        out_shape=jax.ShapeDtypeStruct((rows // 2, 2 * rank), F32),
        in_specs=[VMEM, VMEM],
        out_specs=VMEM,
        scratch_shapes=[pltpu.VMEM((depth, rank), BF16)],
        compiler_params=params(16),
        cost_estimate=pl.CostEstimate(
            flops=2 * rows * depth * rank, bytes_accessed=2 * rows * depth, transcendentals=0
        ),
    )(x, w_t)


def split(x):
    top = x.astype(BF16)
    return top, (x - top.astype(F32)).astype(BF16)


def precise_dot(a, b, dims):
    (top_a, rest_a), (top_b, rest_b) = split(a), split(b)
    axis_a, axis_b = dims
    return lax.dot_general(
        jnp.concatenate([top_a, top_a, rest_a], axis=axis_a),
        jnp.concatenate([top_b, rest_b, top_b], axis=axis_b),
        (((axis_a,), (axis_b,)), ((), ())),
        preferred_element_type=F32,
    )


def outer_kernel(
    length, in_ref, own_ref, got_ref, mask_ref, inv_ref, part_ref, sent_ref, rows_ref, pairs_ref
):
    rank = inv_ref.shape[0]
    seqs = mask_ref.shape[0]
    half = rank // 2
    counts = jnp.sum(mask_ref[...].astype(F32), axis=1, keepdims=True)
    lane = lax.broadcasted_iota(jnp.int32, (length, 2 * rank), 1)
    token = lax.broadcasted_iota(jnp.int32, (length, 2 * rank), 0).astype(F32)
    grams = [None] * seqs
    for pair in range(seqs // 2):
        rows = pl.ds(pair * length, length)
        low, high = counts[pair : pair + 1, :], counts[pair + seqs // 2 : pair + seqs // 2 + 1, :]
        real = token < jnp.where(lane < rank, low, high)
        inside = jnp.where(real, in_ref[rows, :], 0.0)
        outside = own_ref[rows, :] + got_ref[rows, :].astype(F32)
        both = precise_dot(inside, outside, (0, 0))
        grams[pair] = both[:rank, :rank] / low
        grams[pair + seqs // 2] = both[rank:, rank:] / high
    gram = jnp.concatenate(grams, axis=1)
    rows_ref[pl.ds(0, rank), :] = inv_ref[...]
    mixed = jnp.concatenate(
        [rows_ref[pl.ds(0, half, stride=2), :], rows_ref[pl.ds(1, half, stride=2), :]], axis=0
    )
    pre = precise_dot(mixed, gram, (1, 0))
    for s in range(seqs):
        one = pre[:, s * rank : (s + 1) * rank]
        pairs_ref[pl.ds(s * half, half), :] = jnp.concatenate([one[:half], one[half:]], axis=1)
    for b in range(half):
        row = pairs_ref[pl.ds(b, seqs, stride=half), :]
        lanes = pl.ds(b * 2 * rank, 2 * rank)
        part_ref[:, lanes] = row
        sent_ref[:, lanes] = row.astype(BF16)


def outer(in_part, out_own, out_got, token_mask, inv_input):
    seqs, length = token_mask.shape
    rank = inv_input.shape[0]
    shape = (seqs, rank * rank)
    return pl.pallas_call(
        functools.partial(outer_kernel, length),
        out_shape=[jax.ShapeDtypeStruct(shape, F32), jax.ShapeDtypeStruct(shape, BF16)],
        in_specs=[VMEM] * 5,
        out_specs=[VMEM] * 2,
        scratch_shapes=[
            pltpu.VMEM((rank + 16, rank), F32),
            pltpu.VMEM(((seqs + 8) * rank // 2, 2 * rank), F32),
        ],
        compiler_params=params(16),
    )(in_part, out_own, out_got, token_mask, inv_input)


def pass_kernel(x_ref, y_ref):
    y_ref[...] = x_ref[...]


def pass_on(x):
    return pl.pallas_call(
        pass_kernel,
        out_shape=jax.ShapeDtypeStruct(x.shape, x.dtype),
        in_specs=[VMEM],
        out_specs=VMEM,
        compiler_params=params(16),
    )(x)


def score_kernel(place_ref, low_ref, high_ref, *rest):
    *pieces, out_ref, feats_ref = rest
    seqs = pieces[0].shape[0]
    for k, piece in enumerate(pieces):
        feats_ref[pl.ds(k * seqs, seqs), :] = piece[...].astype(F32)
    half = low_ref.shape[1]
    feats = feats_ref[...].astype(BF16)
    scores = lax.dot_general(low_ref[...], feats[:, :half], NT, preferred_element_type=F32)
    scores += lax.dot_general(high_ref[...], feats[:, half:], NT, preferred_element_type=F32)
    scores = scores.T
    rows = scores.shape[0]
    at = lax.broadcasted_iota(jnp.int32, scores.shape, 0)
    size = seqs
    while size < rows:
        swapped = jnp.where(
            (at & size) == 0, pltpu.roll(scores, rows - size, 0), pltpu.roll(scores, size, 0)
        )
        bit = (place_ref[...] & (size // seqs)) != 0
        scores = jnp.where(bit, swapped, scores)
        size *= 2
    out_ref[...] = scores


def score(place, low, high, pieces):
    seqs, feats = pieces[0].shape
    rows = seqs * len(pieces)
    return pl.pallas_call(
        score_kernel,
        out_shape=jax.ShapeDtypeStruct((rows, low.shape[0]), F32),
        in_specs=[VMEM] * (3 + len(pieces)),
        out_specs=VMEM,
        scratch_shapes=[pltpu.VMEM((rows, feats), F32)],
        compiler_params=params(16),
    )(place, low, high, *pieces)


def local_pair(
    activations, out_grads, token_mask, proj_in, proj_out, inv_input, inv_output, query_feats
):
    seqs, length, depth = activations.shape
    ex_size = lax.axis_size("ex")
    ex = lax.axis_index("ex")
    hid = lax.axis_index("hid")
    half = ex_size // 2
    swap_hid = [(0, 1), (1, 0)]

    out_own, out_sent, query_own = project_out(
        out_grads.reshape(seqs * length, -1), proj_out.T, query_feats, inv_output, 4
    )
    out_got = lax.ppermute(out_sent, "hid", swap_hid)
    in_part = project_in(activations.reshape(seqs * length, depth), proj_in.T)
    part, sent = outer(in_part, out_own, out_got, token_mask, inv_input)

    alpha, beta = [], []
    for e in range(half):
        a, b, c, d = 2 * e + 1, 2 * e, 2 * (e + half), 2 * (e + half) + 1
        alpha += [(a, b), (b, c ^ 2), (c, a ^ 2), (d, d ^ 2)]
        beta += [(c, d), (d, a ^ 2), (a, c ^ 2), (b, b ^ 2)]
    axes = ("ex", "hid")
    second = lax.ppermute(sent, axes, beta)
    first = lax.ppermute(sent, axes, alpha)
    home = (ex // half) == hid
    mine = (
        jnp.where(home & (hid == 0), part, second.astype(F32))
        + jnp.where(home & (hid == 1), part, first.astype(F32))
    ).astype(BF16)

    query_own = pass_on(query_own)
    query_got = lax.ppermute(query_own, "hid", swap_hid)
    low = jnp.where(hid == 0, query_own, query_got)
    high = jnp.where(hid == 0, query_got, query_own)

    pieces = {0: mine}
    for k in range(half - 2, 0, -2):
        k = k if k & (k - 1) else k ^ 1
        pieces[k] = lax.ppermute(mine, "ex", [(i, i ^ k) for i in range(ex_size)])
    for k in list(pieces):
        pieces[k ^ 1] = lax.ppermute(pieces[k], "ex", [(i, i ^ 1) for i in range(ex_size)])
    place = jnp.full((seqs * half, query_feats.shape[0]), ex % half ^ jnp.where(home, 0, 1), jnp.int32)
    scores = score(place, low, high, [pieces[k] for k in range(half)])
    return scores.T


def local_any(
    activations, out_grads, token_mask, proj_in, proj_out, inv_input, inv_output, query_feats
):
    seq_count, length, unit_local = activations.shape
    rank_width = proj_in.shape[1]
    hid_size = lax.axis_size("hid")
    row_block = rank_width // hid_size
    my_index = lax.axis_index("hid")
    in_part = jnp.dot(
        activations.reshape(seq_count * length, unit_local),
        proj_in,
        preferred_element_type=F32,
    )
    in_part = jnp.dot(in_part, inv_input, precision=HIGH)
    out_part = jnp.dot(
        out_grads.reshape(seq_count * length, out_grads.shape[2]),
        proj_out,
        preferred_element_type=F32,
    )
    token_weight = token_mask.astype(F32)
    tok_count = jnp.sum(token_weight, axis=1)
    in_full, out_full = lax.psum((in_part, out_part), "hid")
    in_mine = lax.dynamic_slice_in_dim(in_full, my_index * row_block, row_block, 1)
    masked = in_mine.reshape(seq_count, length, row_block) * token_weight[:, :, None]
    outer_sum = jnp.einsum(
        "slr,slq->srq",
        masked,
        out_full.reshape(seq_count, length, rank_width),
        precision=HIGH,
    )
    train_feats = (
        (outer_sum / tok_count[:, None, None])
        .astype(BF16)
        .reshape(seq_count, row_block * rank_width)
    )
    query_count = query_feats.shape[0]
    queries = query_feats.reshape(query_count, row_block, rank_width).astype(F32)
    query_pre = jnp.einsum("qij,jk->qik", queries, inv_output, precision=HIGH)
    query_pre = query_pre.astype(BF16).reshape(query_count, row_block * rank_width)
    partial_value = jnp.einsum(
        "qk,tk->qt",
        query_pre,
        lax.all_gather(train_feats, "ex", axis=0, tiled=True),
        preferred_element_type=F32,
    )
    return lax.psum_scatter(partial_value, "hid", scatter_dimension=1, tiled=True)


def solution(mesh):
    ex_size, hid_size = mesh.shape["ex"], mesh.shape["hid"]
    paired = hid_size == 2 and ex_size >= 4 and ex_size & (ex_size - 1) == 0
    return jax.shard_map(
        local_pair if paired else local_any,
        mesh=mesh,
        in_specs=(
            P("ex", None, "hid"),
            P("ex", None, "hid"),
            P("ex", None),
            P("hid", None),
            P("hid", None),
            P(),
            P(),
            P("ex", "hid"),
        ),
        out_specs=P("ex", "hid"),
        check_vma=False,
    )
```

```python
import functools

import jax
import jax.numpy as jnp
from jax import lax
from jax.experimental import pallas as pl
from jax.experimental.pallas import tpu as pltpu
from jax.sharding import PartitionSpec as P

F32 = jnp.float32
BF16 = jnp.bfloat16
NT = (((1,), (1,)), ((), ()))
TN = (((0,), (0,)), ((), ()))
VMEM = pl.BlockSpec(memory_space=pltpu.VMEM)
HBM = pl.BlockSpec(memory_space=pltpu.HBM)
HIGH = lax.Precision.HIGHEST


def params(mib):
    return pltpu.CompilerParams(vmem_limit_bytes=mib << 20)


def hbm(x):
    return pltpu.with_memory_space_constraint(x, pltpu.HBM)


def precondition(query_ref, inv_ref, block_ref, pre_ref):
    rank = inv_ref.shape[0]
    block_ref[...] = jnp.zeros_like(block_ref)
    block_ref[pl.ds(0, rank), pl.ds(0, rank)] = inv_ref[...]
    block_ref[pl.ds(rank, rank), pl.ds(rank, rank)] = inv_ref[...]
    block = block_ref[...]
    top = block.astype(BF16)
    rest = block - top.astype(F32)
    middle = rest.astype(BF16)
    last = (rest - middle.astype(F32)).astype(BF16)
    count, feats = query_ref.shape
    width = 2 * rank
    tiles = feats // width
    stacked = jnp.concatenate(
        [query_ref[:, b * width : (b + 1) * width] for b in range(tiles)], axis=0
    )
    terms = jnp.dot(
        stacked, jnp.concatenate([last, middle, top], axis=1), preferred_element_type=F32
    )
    total = terms[:, :width] + terms[:, width : 2 * width] + terms[:, 2 * width :]
    for b in range(tiles):
        tile = total[b * count : (b + 1) * count]
        pre_ref[:, pl.ds(b * width, width)] = tile.astype(BF16)


def out_kernel(
    chunks, x_hbm, w_hbm, query_hbm, inv_hbm, out_ref, sent_ref, pre_ref,
    x_ref, wide_ref, tall_ref, query_ref, inv_ref, block_ref, sems,
):
    rows = x_hbm.shape[0]
    step = rows // chunks
    weights = pltpu.make_async_copy(w_hbm, wide_ref, sems.at[chunks])
    inverse = pltpu.make_async_copy(inv_hbm, inv_ref, sems.at[chunks + 1])
    queries = pltpu.make_async_copy(query_hbm, query_ref, sems.at[chunks + 2])
    inverse.start()
    queries.start()
    weights.start()
    copies = [
        pltpu.make_async_copy(
            x_hbm.at[pl.ds(c * step, step)], x_ref.at[pl.ds(c * step, step)], sems.at[c]
        )
        for c in range(chunks)
    ]
    for copy in copies:
        copy.start()
    inverse.wait()
    queries.wait()
    precondition(query_ref, inv_ref, block_ref, pre_ref)
    weights.wait()
    tall_ref[...] = wide_ref[...].T
    half = rows // 2
    rank = w_hbm.shape[0]
    for side in range(2):
        for copy in copies[side * chunks // 2 : (side + 1) * chunks // 2]:
            copy.wait()
        part = jnp.dot(
            x_ref[pl.ds(side * half, half), :], tall_ref[...], preferred_element_type=F32
        )
        out_ref[:, pl.ds(side * rank, rank)] = part
        sent_ref[:, pl.ds(side * rank, rank)] = part.astype(BF16)


def project_out(x, w_t, query, inv, chunks):
    rows, depth = x.shape
    rank = w_t.shape[0]
    shape = (rows // 2, 2 * rank)
    return pl.pallas_call(
        functools.partial(out_kernel, chunks),
        out_shape=[
            jax.ShapeDtypeStruct(shape, F32),
            jax.ShapeDtypeStruct(shape, BF16),
            jax.ShapeDtypeStruct(query.shape, BF16),
        ],
        in_specs=[HBM] * 4,
        out_specs=[VMEM] * 3,
        scratch_shapes=[
            pltpu.VMEM((rows, depth), BF16),
            pltpu.VMEM((rank, depth), BF16),
            pltpu.VMEM((depth, rank), BF16),
            pltpu.VMEM(query.shape, BF16),
            pltpu.VMEM(inv.shape, F32),
            pltpu.VMEM((2 * rank, 2 * rank), F32),
            pltpu.SemaphoreType.DMA((chunks + 3,)),
        ],
        compiler_params=params(16),
        cost_estimate=pl.CostEstimate(
            flops=60 * rows * depth * rank, bytes_accessed=60 * rows * depth, transcendentals=0
        ),
    )(hbm(x), hbm(w_t), hbm(query), hbm(inv))


def in_kernel(x_ref, w_ref, out_ref, tall_ref):
    half = x_ref.shape[0] // 2
    rank = w_ref.shape[0]
    tall_ref[...] = w_ref[...].T
    for side in range(2):
        part = jnp.dot(
            x_ref[pl.ds(side * half, half), :], tall_ref[...], preferred_element_type=F32
        )
        out_ref[:, pl.ds(side * rank, rank)] = part


def project_in(x, w_t):
    rows, depth = x.shape
    rank = w_t.shape[0]
    return pl.pallas_call(
        in_kernel,
        out_shape=jax.ShapeDtypeStruct((rows // 2, 2 * rank), F32),
        in_specs=[VMEM, VMEM],
        out_specs=VMEM,
        scratch_shapes=[pltpu.VMEM((depth, rank), BF16)],
        compiler_params=params(16),
        cost_estimate=pl.CostEstimate(
            flops=2 * rows * depth * rank, bytes_accessed=2 * rows * depth, transcendentals=0
        ),
    )(x, w_t)


def split(x):
    top = x.astype(BF16)
    return top, (x - top.astype(F32)).astype(BF16)


def precise_dot(a, b, dims):
    (top_a, rest_a), (top_b, rest_b) = split(a), split(b)
    axis_a, axis_b = dims
    return lax.dot_general(
        jnp.concatenate([top_a, top_a, rest_a], axis=axis_a),
        jnp.concatenate([top_b, rest_b, top_b], axis=axis_b),
        (((axis_a,), (axis_b,)), ((), ())),
        preferred_element_type=F32,
    )


def outer_kernel(
    length, in_ref, own_ref, got_ref, mask_ref, inv_ref, part_ref, sent_ref, rows_ref, pairs_ref
):
    rank = inv_ref.shape[0]
    seqs = mask_ref.shape[0]
    half = rank // 2
    counts = jnp.sum(mask_ref[...].astype(F32), axis=1, keepdims=True)
    lane = lax.broadcasted_iota(jnp.int32, (length, 2 * rank), 1)
    token = lax.broadcasted_iota(jnp.int32, (length, 2 * rank), 0).astype(F32)
    grams = [None] * seqs
    for pair in range(seqs // 2):
        rows = pl.ds(pair * length, length)
        low, high = counts[pair : pair + 1, :], counts[pair + seqs // 2 : pair + seqs // 2 + 1, :]
        real = token < jnp.where(lane < rank, low, high)
        inside = jnp.where(real, in_ref[rows, :], 0.0)
        outside = own_ref[rows, :] + got_ref[rows, :].astype(F32)
        both = precise_dot(inside, outside, (0, 0))
        grams[pair] = both[:rank, :rank] / low
        grams[pair + seqs // 2] = both[rank:, rank:] / high
    gram = jnp.concatenate(grams, axis=1)
    rows_ref[pl.ds(0, rank), :] = inv_ref[...]
    mixed = jnp.concatenate(
        [rows_ref[pl.ds(0, half, stride=2), :], rows_ref[pl.ds(1, half, stride=2), :]], axis=0
    )
    pre = precise_dot(mixed, gram, (1, 0))
    for s in range(seqs):
        one = pre[:, s * rank : (s + 1) * rank]
        pairs_ref[pl.ds(s * half, half), :] = jnp.concatenate([one[:half], one[half:]], axis=1)
    for b in range(half):
        row = pairs_ref[pl.ds(b, seqs, stride=half), :]
        lanes = pl.ds(b * 2 * rank, 2 * rank)
        part_ref[:, lanes] = row
        sent_ref[:, lanes] = row.astype(BF16)


def outer(in_part, out_own, out_got, token_mask, inv_input):
    seqs, length = token_mask.shape
    rank = inv_input.shape[0]
    shape = (seqs, rank * rank)
    return pl.pallas_call(
        functools.partial(outer_kernel, length),
        out_shape=[jax.ShapeDtypeStruct(shape, F32), jax.ShapeDtypeStruct(shape, BF16)],
        in_specs=[VMEM] * 5,
        out_specs=[VMEM] * 2,
        scratch_shapes=[
            pltpu.VMEM((rank + 16, rank), F32),
            pltpu.VMEM(((seqs + 8) * rank // 2, 2 * rank), F32),
        ],
        compiler_params=params(16),
    )(in_part, out_own, out_got, token_mask, inv_input)


def pass_kernel(x_ref, y_ref):
    y_ref[...] = x_ref[...]


def pass_on(x):
    return pl.pallas_call(
        pass_kernel,
        out_shape=jax.ShapeDtypeStruct(x.shape, x.dtype),
        in_specs=[VMEM],
        out_specs=VMEM,
        compiler_params=params(16),
    )(x)


def score_kernel(place_ref, low_ref, high_ref, *rest):
    *pieces, out_ref, feats_ref = rest
    seqs = pieces[0].shape[0]
    for k, piece in enumerate(pieces):
        feats_ref[pl.ds(k * seqs, seqs), :] = piece[...].astype(F32)
    half = low_ref.shape[1]
    feats = feats_ref[...].astype(BF16)
    scores = lax.dot_general(low_ref[...], feats[:, :half], NT, preferred_element_type=F32)
    scores += lax.dot_general(high_ref[...], feats[:, half:], NT, preferred_element_type=F32)
    scores = scores.T
    rows = scores.shape[0]
    at = lax.broadcasted_iota(jnp.int32, scores.shape, 0)
    size = seqs
    while size < rows:
        swapped = jnp.where(
            (at & size) == 0, pltpu.roll(scores, rows - size, 0), pltpu.roll(scores, size, 0)
        )
        bit = (place_ref[...] & (size // seqs)) != 0
        scores = jnp.where(bit, swapped, scores)
        size *= 2
    out_ref[...] = scores


def score(place, low, high, pieces):
    seqs, feats = pieces[0].shape
    rows = seqs * len(pieces)
    return pl.pallas_call(
        score_kernel,
        out_shape=jax.ShapeDtypeStruct((rows, low.shape[0]), F32),
        in_specs=[VMEM] * (3 + len(pieces)),
        out_specs=VMEM,
        scratch_shapes=[pltpu.VMEM((rows, feats), F32)],
        compiler_params=params(16),
    )(place, low, high, *pieces)


def local_pair(
    activations, out_grads, token_mask, proj_in, proj_out, inv_input, inv_output, query_feats
):
    seqs, length, depth = activations.shape
    ex_size = lax.axis_size("ex")
    ex = lax.axis_index("ex")
    hid = lax.axis_index("hid")
    half = ex_size // 2
    swap_hid = [(0, 1), (1, 0)]

    out_own, out_sent, query_own = project_out(
        out_grads.reshape(seqs * length, -1), proj_out.T, query_feats, inv_output, 2
    )
    out_got = lax.ppermute(out_sent, "hid", swap_hid)
    in_part = project_in(activations.reshape(seqs * length, depth), proj_in.T)
    part, sent = outer(in_part, out_own, out_got, token_mask, inv_input)

    alpha, beta = [], []
    for e in range(half):
        a, b, c, d = 2 * e + 1, 2 * e, 2 * (e + half), 2 * (e + half) + 1
        alpha += [(a, b), (b, c ^ 2), (c, a ^ 2), (d, d ^ 2)]
        beta += [(c, d), (d, a ^ 2), (a, c ^ 2), (b, b ^ 2)]
    axes = ("ex", "hid")
    second = lax.ppermute(sent, axes, beta)
    first = lax.ppermute(sent, axes, alpha)
    home = (ex // half) == hid
    mine = (
        jnp.where(home & (hid == 0), part, second.astype(F32))
        + jnp.where(home & (hid == 1), part, first.astype(F32))
    ).astype(BF16)

    query_own = pass_on(query_own)
    query_got = lax.ppermute(query_own, "hid", swap_hid)
    low = jnp.where(hid == 0, query_own, query_got)
    high = jnp.where(hid == 0, query_got, query_own)

    pieces = {0: mine}
    for k in range(half - 2, 0, -2):
        k = k if k & (k - 1) else k ^ 1
        pieces[k] = lax.ppermute(mine, "ex", [(i, i ^ k) for i in range(ex_size)])
    for k in list(pieces):
        pieces[k ^ 1] = lax.ppermute(pieces[k], "ex", [(i, i ^ 1) for i in range(ex_size)])
    place = jnp.full((seqs * half, query_feats.shape[0]), ex % half ^ jnp.where(home, 0, 1), jnp.int32)
    scores = score(place, low, high, [pieces[k] for k in range(half)])
    return scores.T


def local_any(
    activations, out_grads, token_mask, proj_in, proj_out, inv_input, inv_output, query_feats
):
    seq_count, length, unit_local = activations.shape
    rank_width = proj_in.shape[1]
    hid_size = lax.axis_size("hid")
    row_block = rank_width // hid_size
    my_index = lax.axis_index("hid")
    in_part = jnp.dot(
        activations.reshape(seq_count * length, unit_local),
        proj_in,
        preferred_element_type=F32,
    )
    in_part = jnp.dot(in_part, inv_input, precision=HIGH)
    out_part = jnp.dot(
        out_grads.reshape(seq_count * length, out_grads.shape[2]),
        proj_out,
        preferred_element_type=F32,
    )
    token_weight = token_mask.astype(F32)
    tok_count = jnp.sum(token_weight, axis=1)
    in_full, out_full = lax.psum((in_part, out_part), "hid")
    in_mine = lax.dynamic_slice_in_dim(in_full, my_index * row_block, row_block, 1)
    masked = in_mine.reshape(seq_count, length, row_block) * token_weight[:, :, None]
    outer_sum = jnp.einsum(
        "slr,slq->srq",
        masked,
        out_full.reshape(seq_count, length, rank_width),
        precision=HIGH,
    )
    train_feats = (
        (outer_sum / tok_count[:, None, None])
        .astype(BF16)
        .reshape(seq_count, row_block * rank_width)
    )
    query_count = query_feats.shape[0]
    queries = query_feats.reshape(query_count, row_block, rank_width).astype(F32)
    query_pre = jnp.einsum("qij,jk->qik", queries, inv_output, precision=HIGH)
    query_pre = query_pre.astype(BF16).reshape(query_count, row_block * rank_width)
    partial_value = jnp.einsum(
        "qk,tk->qt",
        query_pre,
        lax.all_gather(train_feats, "ex", axis=0, tiled=True),
        preferred_element_type=F32,
    )
    return lax.psum_scatter(partial_value, "hid", scatter_dimension=1, tiled=True)


def solution(mesh):
    ex_size, hid_size = mesh.shape["ex"], mesh.shape["hid"]
    paired = hid_size == 2 and ex_size >= 4 and ex_size & (ex_size - 1) == 0
    return jax.shard_map(
        local_pair if paired else local_any,
        mesh=mesh,
        in_specs=(
            P("ex", None, "hid"),
            P("ex", None, "hid"),
            P("ex", None),
            P("hid", None),
            P("hid", None),
            P(),
            P(),
            P("ex", "hid"),
        ),
        out_specs=P("ex", "hid"),
        check_vma=False,
    )
```
